512 devices in a mesh: dp: 512 (over x, y, z, core).
Axes of the slice: x: 4, y: 4, z: 16, core: 2. Of those that a mesh axis runs over, the one named last changes fastest.
Arguments:
- image_embed: bfloat16 [262144, 768], P('dp'), may hold values from -1.5 to 1.5
- text_embed: bfloat16 [262144, 768], P('dp'), may hold values from -1.5 to 1.5
- logit_scale: float32 [1], replicated, may hold values from 1 to 3
- logit_bias: float32 [1], replicated, may hold values from -3 to 0
Outputs:
- row_loss: float32 [262144], P('dp')
- grad_image: float32 [262144, 768], P('dp')
- grad_text: float32 [262144, 768], P('dp')
The draws below stay inside these ranges and needn't reach their ends.
All inputs are finite; a program needn't handle non-finite values.
Results may differ from the reference program's by a relative error of at most 0.0022.
Values may be sent and summed in bfloat16 or wider, within the bound.
A program may use at most 64 MiB of HBM per device.

```python
import jax
import jax.numpy as jnp
from jax import lax

D = 768
ROWS = 512
TOKENS = 262144


def block_levels(own_key, extent, cuts, least, high):
    factor_of = 1.0
    for position, shards_of in cuts:
        draws = jax.random.uniform(jax.random.fold_in(jax.random.fold_in(own_key, 6), position), (shards_of,), jnp.float32, least / len(cuts), high / len(cuts))
        factor_of = factor_of * jnp.repeat(jnp.exp(draws), extent[position] // shards_of).reshape((-1,) + (1,) * (len(extent) - 1 - position))
    return factor_of


def normal_values(rng, dims, scale, reach, cuts=(), kind=jnp.bfloat16):
    entries = jax.random.normal(rng, dims, jnp.float32) * scale
    if len(cuts) > 0:
        entries = block_levels(rng, dims, cuts, -0.22, 0.18) * entries
    return jnp.clip(entries, min=-reach, max=reach).astype(kind)


def setup_inputs(seed: int = 0) -> dict:
    streams_of = jax.random.split(jax.random.key(seed), 5)
    return {
        "image_embed": normal_values(streams_of[0], (TOKENS, D), 0.25, 1.5, ((0, 512),)),
        "text_embed": normal_values(streams_of[1], (TOKENS, D), 0.25, 1.5, ((0, 512),)),
        "logit_scale": jnp.clip(jax.random.uniform(streams_of[2], (1,), jnp.float32, 1.0, 3.0), 1.0, 3.0),
        "logit_bias": jnp.clip(jax.random.uniform(streams_of[3], (1,), jnp.float32, -3.0, 0.0), -3.0, 0.0),
    }


def score_block(images, texts, scale, bias, labels):
    inner = jnp.dot(images, texts.T, preferred_element_type=jnp.float32)
    logits = scale * inner + bias
    losses = jnp.sum(jax.nn.softplus(-labels * logits), axis=1)
    positive = (labels > 0.0).astype(jnp.float32)
    coeff = (scale * (jax.nn.sigmoid(logits) - positive)).astype(jnp.bfloat16)
    grad_rows = jnp.dot(coeff, texts, preferred_element_type=jnp.float32)
    partial_cols = jnp.dot(coeff.T, images, preferred_element_type=jnp.float32)
    return losses, grad_rows, partial_cols


def reference(image_embed, text_embed, logit_scale, logit_bias):
    count = image_embed.shape[0] // ROWS
    width = image_embed.shape[1]
    image_blocks = image_embed.reshape(count, ROWS, width)
    text_blocks = text_embed.reshape(count, ROWS, width)
    text_near = jnp.roll(text_blocks, 1, axis=0)
    text_far = jnp.roll(text_blocks, 2, axis=0)
    scale = logit_scale[0]
    bias = logit_bias[0]
    eye = jnp.eye(ROWS, dtype=jnp.float32)
    own_labels = 2.0 * eye - 1.0
    other_labels = -jnp.ones((ROWS, ROWS), jnp.float32)

    def one_block(items):
        images, own, near, far = items
        loss_a, grad_a, part_a = score_block(images, own, scale, bias, own_labels)
        loss_b, grad_b, part_b = score_block(images, near, scale, bias, other_labels)
        loss_c, grad_c, part_c = score_block(images, far, scale, bias, other_labels)
        losses = (loss_a + loss_b + loss_c) / (3.0 * ROWS)
        return losses, grad_a + grad_b + grad_c, part_a, part_b, part_c

    losses, grads, part_own, part_near, part_far = lax.map(one_block, (image_blocks, text_blocks, text_near, text_far))
    grad_text = part_own + jnp.roll(part_near, -1, axis=0) + jnp.roll(part_far, -2, axis=0)
    return losses.reshape(-1), grads.reshape(-1, width), grad_text.reshape(-1, width)
```

```python
import functools

import jax
import jax.numpy as jnp
from jax import lax
from jax.experimental import pallas as pl
from jax.experimental.pallas import tpu as pltpu
from jax.sharding import PartitionSpec as P

MESH = pl.DeviceIdType.MESH
PARTS = 4
WIDE = 256
NT = (((1,), (1,)), ((), ()))


def work(own, other, acc, loss, scale, bias, diagonal=None):
    columns = other.shape[0]
    logits = scale * lax.dot_general(own, other, NT, preferred_element_type=jnp.float32) + bias
    small = jnp.exp(-jnp.abs(logits))
    inverse = 1.0 / (1.0 + small)
    sigmoid = jnp.where(logits >= 0.0, inverse, small * inverse)
    signed = logits
    if diagonal is not None:
        rows = lax.broadcasted_iota(jnp.int32, logits.shape, 0)
        match = lax.broadcasted_iota(jnp.int32, logits.shape, 1) + diagonal == rows
        sigmoid = sigmoid - jnp.where(match, 1.0, 0.0)
        signed = jnp.where(match, -logits, logits)
    losses = jnp.maximum(signed, 0.0) + jnp.log1p(small)
    coeff = (scale * sigmoid).astype(jnp.bfloat16)
    acc[...] += jnp.dot(coeff, other, preferred_element_type=jnp.float32)
    total = losses[:, 0:128]
    for first in range(128, columns, 128):
        total += losses[:, first:first + 128]
    loss[...] += total


def kernel(devices, image_ref, text_ref, scale_ref, bias_ref, loss_ref, gimage_ref, gtext_ref,
           x, y, z1, z2, w1, w2, accx, accy, lossx, lossy, load_sem, out_sem, send, recv):
    me = lax.axis_index("dp")
    core = lax.rem(me, 2)
    step = 2 * core - 1
    partner = me - step
    near = lax.rem(me + step + devices, devices)
    far = lax.rem(me + 2 * step + devices, devices)
    behind = lax.rem(me - 2 * step + devices, devices)
    rows = x.shape[0]
    part = rows // PARTS

    barrier = pltpu.get_barrier_semaphore()
    for other in (partner, near, far, behind):
        pl.semaphore_signal(barrier, inc=1, device_id=(other,), device_id_type=MESH)

    def load(source, target, slot):
        return pltpu.make_async_copy(source, target, load_sem.at[slot])

    @pl.when(core == 1)
    def _():
        load(text_ref, x, 0).start()
        load(image_ref, y, 1).start()

    @pl.when(core == 0)
    def _():
        load(image_ref, x, 0).start()
        load(text_ref, y, 1).start()

    accx[...] = jnp.zeros_like(accx)
    accy[...] = jnp.zeros_like(accy)
    lossx[...] = jnp.zeros_like(lossx)
    lossy[...] = jnp.zeros_like(lossy)
    scale = scale_ref[0]
    bias = bias_ref[0]
    load(image_ref, x, 0).wait()
    load(text_ref, y, 1).wait()

    def remote(source, target, way, index, device):
        piece = pl.ds(pl.multiple_of(index * part, part), part)
        return pltpu.make_async_remote_copy(
            src_ref=source.at[piece], dst_ref=target.at[piece], send_sem=send.at[way, index],
            recv_sem=recv.at[way, index], device_id=(device,), device_id_type=MESH)

    def to_partner(index):
        return remote(y, z1, 0, index, partner)

    def to_far(index):
        return remote(x, z2, 1, index, far)

    def to_near(index):
        return remote(z1, w2, 2, index, near)

    def relay(index):
        return remote(z2, w1, 3, index, partner)

    def each(action):
        def run(index, carry):
            action(index)
            return carry
        lax.fori_loop(0, PARTS, run, 0)

    pl.semaphore_wait(barrier, 4)
    each(lambda index: to_far(index).start())
    each(lambda index: to_partner(index).start())

    def wide(action):
        def run(index, carry):
            start = pl.multiple_of(index * WIDE, WIDE)
            action(start, pl.ds(start, WIDE))
            return carry
        lax.fori_loop(0, rows // WIDE, run, 0)

    wide(lambda start, piece: work(y[...], x[piece, :], accy, lossy, scale, bias, start))
    wide(lambda start, piece: work(x[...], y[piece, :], accx, lossx, scale, bias, start))

    def forward(index):
        to_partner(index).wait_recv()
        to_near(index).start()

    each(forward)
    wide(lambda start, piece: work(y[...], z1[piece, :], accy, lossy, scale, bias))

    def visiting(index):
        piece = pl.ds(pl.multiple_of(index * part, part), part)
        to_far(index).wait_recv()
        relay(index).start()
        work(y[...], z2[piece, :], accy, lossy, scale, bias)
        relay(index).wait_recv()
        work(x[...], w1[piece, :], accx, lossx, scale, bias)

    each(visiting)

    def store(source, target, slot):
        return pltpu.make_async_copy(source, target, out_sem.at[slot])

    @pl.when(core == 1)
    def _():
        store(accy, gimage_ref, 0).start()

    @pl.when(core == 0)
    def _():
        store(accy, gtext_ref, 0).start()

    def last(index):
        piece = pl.ds(pl.multiple_of(index * part, part), part)
        to_near(index).wait_recv()
        work(x[...], w2[piece, :], accx, lossx, scale, bias)

    each(last)

    @pl.when(core == 1)
    def _():
        store(accx, gtext_ref, 1).start()

    @pl.when(core == 0)
    def _():
        store(accx, gimage_ref, 1).start()

    lanes = jnp.where(core == 1, lossy[...], lossx[...])
    loss_ref[...] = jnp.sum(lanes.T, axis=0, keepdims=True) / (3.0 * rows)

    def drain(index):
        to_partner(index).wait_send()
        to_far(index).wait_send()
        to_near(index).wait_send()
        relay(index).wait_send()

    each(drain)
    store(accy, gimage_ref, 0).wait()
    store(accx, gtext_ref, 1).wait()


def body(image_embed, text_embed, logit_scale, logit_bias):
    rows, width = image_embed.shape
    devices = lax.axis_size("dp")
    block = pltpu.VMEM((rows, width), jnp.bfloat16)
    wide = pltpu.VMEM((rows, width), jnp.float32)
    lanes = pltpu.VMEM((rows, 128), jnp.float32)
    hbm = pl.BlockSpec(memory_space=pl.ANY)
    smem = pl.BlockSpec(memory_space=pltpu.SMEM)
    loss, grad_image, grad_text = pl.pallas_call(
        functools.partial(kernel, devices),
        out_shape=(
            jax.ShapeDtypeStruct((1, rows), jnp.float32),
            jax.ShapeDtypeStruct((rows, width), jnp.float32),
            jax.ShapeDtypeStruct((rows, width), jnp.float32),
        ),
        in_specs=[hbm, hbm, smem, smem],
        out_specs=(pl.BlockSpec(memory_space=pltpu.VMEM), hbm, hbm),
        scratch_shapes=[
            block, block, block, block, block, block, wide, wide, lanes, lanes,
            pltpu.SemaphoreType.DMA((2,)), pltpu.SemaphoreType.DMA((2,)),
            pltpu.SemaphoreType.DMA((4, PARTS)), pltpu.SemaphoreType.DMA((4, PARTS)),
        ],
        compiler_params=pltpu.CompilerParams(
            collective_id=0, has_side_effects=True, vmem_limit_bytes=48 << 20),
        name="sigmoid_ring",
    )(image_embed, text_embed, logit_scale, logit_bias)
    return loss.reshape(rows), grad_image, grad_text


def solution(mesh):
    in_specs = (P("dp", None), P("dp", None), P(), P())
    out_specs = (P("dp"), P("dp", None), P("dp", None))
    return jax.shard_map(body, mesh=mesh, in_specs=in_specs, out_specs=out_specs, check_vma=False)
```

```python
import functools

import jax
import jax.numpy as jnp
from jax import lax
from jax.experimental import pallas as pl
from jax.experimental.pallas import tpu as pltpu
from jax.sharding import PartitionSpec as P

MESH = pl.DeviceIdType.MESH
PARTS = 4
WIDE = 256
GATE = 2
NT = (((1,), (1,)), ((), ()))
PARTNER, DIRECT, RELAYED, SECOND = 0, 1, 2, 3


def work(own, other, acc, loss, scale, bias, diagonal=None):
    columns = other.shape[0]
    logits = scale * lax.dot_general(own, other, NT, preferred_element_type=jnp.float32) + bias
    small = jnp.exp(-jnp.abs(logits))
    inverse = 1.0 / (1.0 + small)
    sigmoid = jnp.where(logits >= 0.0, inverse, small * inverse)
    signed = logits
    if diagonal is not None:
        rows = lax.broadcasted_iota(jnp.int32, logits.shape, 0)
        match = lax.broadcasted_iota(jnp.int32, logits.shape, 1) + diagonal == rows
        sigmoid = sigmoid - jnp.where(match, 1.0, 0.0)
        signed = jnp.where(match, -logits, logits)
    losses = jnp.maximum(signed, 0.0) + jnp.log1p(small)
    coeff = (scale * sigmoid).astype(jnp.bfloat16)
    acc[...] += jnp.dot(coeff, other, preferred_element_type=jnp.float32)
    total = losses[:, 0:128]
    for first in range(128, columns, 128):
        total += losses[:, first:first + 128]
    loss[...] += total


def ring_kernel(devices, image_ref, text_ref, scale_ref, bias_ref, acc, loss,
                own, blocks, load_sem, send, recv, ready):
    me = lax.axis_index("dp")
    core = lax.rem(me, 2)
    step = 2 * core - 1
    partner = me - step
    near = lax.rem(me + step + devices, devices)
    far = lax.rem(me + 2 * step + devices, devices)
    rows = own.shape[1]
    part = rows // PARTS

    barrier = pltpu.get_barrier_semaphore()
    previous = lax.rem(me - 1 - core + devices, devices)
    for other in (partner, previous):
        pl.semaphore_signal(barrier, inc=1, device_id=(other,), device_id_type=MESH)

    def load(source, target, slot):
        return pltpu.make_async_copy(source, target, load_sem.at[slot])

    load(image_ref, own.at[0], 0).start()
    load(text_ref, own.at[1], 1).start()
    acc[...] = jnp.zeros_like(acc)
    loss[...] = jnp.zeros_like(loss)
    scale = scale_ref[0]
    bias = bias_ref[0]
    load(image_ref, own.at[0], 0).wait()
    load(text_ref, own.at[1], 1).wait()

    def piece_of(index):
        return pl.ds(pl.multiple_of(index * part, part), part)

    def remote(source, way, index, device):
        return pltpu.make_async_remote_copy(
            src_ref=source.at[piece_of(index)], dst_ref=blocks.at[way, piece_of(index)],
            send_sem=send.at[way, index], recv_sem=recv.at[way, index],
            device_id=(device,), device_id_type=MESH)

    def to_partner(index):
        return remote(own.at[1 - core], PARTNER, index, partner)

    def to_far(index):
        return remote(own.at[core], DIRECT, index, far)

    def relay(index):
        return remote(blocks.at[DIRECT], RELAYED, index, partner)

    def to_near(index):
        return remote(blocks.at[PARTNER], SECOND, index, near)

    def each(action, first=0, last=PARTS):
        def run(index, carry):
            action(index)
            return carry
        lax.fori_loop(first, last, run, 0)

    @pl.when(core == 1)
    def _():
        pl.semaphore_wait(barrier, 3)
        pl.semaphore_signal(ready, inc=1, device_id=(near,), device_id_type=MESH)

    @pl.when(core == 0)
    def _():
        pl.semaphore_wait(barrier, 1)

    each(lambda index: to_partner(index).start())

    @pl.when(core == 0)
    def _():
        pl.semaphore_wait(ready, 1)

    each(lambda index: to_far(index).start())

    def wide(action):
        def run(index, carry):
            start = pl.multiple_of(index * WIDE, WIDE)
            action(start, pl.ds(start, WIDE))
            return carry
        lax.fori_loop(0, rows // WIDE, run, 0)

    wide(lambda start, piece: work(own[0], own[1, piece], acc.at[0], loss.at[0], scale, bias, start))
    wide(lambda start, piece: work(own[1], own[0, piece], acc.at[1], loss.at[1], scale, bias, start))

    each(lambda index: to_far(index).wait_send(), 0, GATE)

    def forward(index):
        to_partner(index).wait_recv()
        to_near(index).start()

    each(forward)
    wide(lambda start, piece: work(
        own[1 - core], blocks[PARTNER, piece], acc.at[1 - core], loss.at[1 - core], scale, bias))

    def visit(index, carry):
        phase = lax.div(index, PARTS)
        chunk = lax.rem(index, PARTS)
        slot = 1 + phase
        side = jnp.where(slot == DIRECT, 1 - core, core)
        piece = piece_of(chunk)
        pltpu.make_async_remote_copy(
            src_ref=blocks.at[slot, piece], dst_ref=blocks.at[slot, piece],
            send_sem=send.at[slot, chunk], recv_sem=recv.at[slot, chunk],
            device_id=(partner,), device_id_type=MESH).wait_recv()

        @pl.when(slot == DIRECT)
        def _():
            relay(chunk).start()

        work(own[side], blocks[slot, piece], acc.at[side], loss.at[side], scale, bias)
        return carry

    lax.fori_loop(0, 3 * PARTS, visit, 0)

    each(lambda index: to_far(index).wait_send(), GATE)

    def drain(index):
        to_partner(index).wait_send()
        to_near(index).wait_send()
        relay(index).wait_send()

    each(drain)


def finish_kernel(acc, loss, loss_ref, image_ref, text_ref, sems):
    rows = loss.shape[1]
    stores = [
        pltpu.make_async_copy(acc.at[side], target, sems.at[side])
        for side, target in ((0, image_ref), (1, text_ref))
    ]
    for store in stores:
        store.start()
    loss_ref[...] = jnp.sum(loss[0].T, axis=0, keepdims=True) / (3.0 * rows)
    for store in stores:
        store.wait()


def body(image_embed, text_embed, logit_scale, logit_bias):
    rows, width = image_embed.shape
    devices = lax.axis_size("dp")
    anywhere = pl.BlockSpec(memory_space=pl.ANY)
    smem = pl.BlockSpec(memory_space=pltpu.SMEM)
    hbm = pl.BlockSpec(memory_space=pltpu.HBM)
    vmem = pl.BlockSpec(memory_space=pltpu.VMEM)
    image_embed, text_embed = (pltpu.with_memory_space_constraint(a, pltpu.HBM) for a in (image_embed, text_embed))
    acc, loss = pl.pallas_call(
        functools.partial(ring_kernel, devices),
        out_shape=(
            pltpu.VMEM((2, rows, width), jnp.float32),
            pltpu.VMEM((2, rows, 128), jnp.float32),
        ),
        in_specs=[hbm, hbm, smem, smem],
        out_specs=(vmem, vmem),
        scratch_shapes=[
            pltpu.VMEM((2, rows, width), jnp.bfloat16),
            pltpu.VMEM((4, rows, width), jnp.bfloat16),
            pltpu.SemaphoreType.DMA((2,)),
            pltpu.SemaphoreType.DMA((4, PARTS)),
            pltpu.SemaphoreType.DMA((4, PARTS)),
            pltpu.SemaphoreType.REGULAR,
        ],
        compiler_params=pltpu.CompilerParams(
            collective_id=0, has_side_effects=True, vmem_limit_bytes=32 << 20),
        name="sigmoid_ring",
    )(image_embed, text_embed, logit_scale, logit_bias)
    acc, loss = (pltpu.with_memory_space_constraint(a, pltpu.VMEM) for a in (acc, loss))
    row_loss, grad_image, grad_text = pl.pallas_call(
        finish_kernel,
        out_shape=(
            jax.ShapeDtypeStruct((1, rows), jnp.float32),
            jax.ShapeDtypeStruct((rows, width), jnp.float32),
            jax.ShapeDtypeStruct((rows, width), jnp.float32),
        ),
        in_specs=[vmem, vmem],
        out_specs=(vmem, anywhere, anywhere),
        scratch_shapes=[pltpu.SemaphoreType.DMA((2,))],
        compiler_params=pltpu.CompilerParams(vmem_limit_bytes=4 << 20),
        name="finish",
    )(acc, loss)
    return row_loss.reshape(rows), grad_image, grad_text


def solution(mesh):
    in_specs = (P("dp", None), P("dp", None), P(), P())
    out_specs = (P("dp"), P("dp", None), P("dp", None))
    return jax.shard_map(body, mesh=mesh, in_specs=in_specs, out_specs=out_specs, check_vma=False)
```

```python
import functools

import jax
import jax.numpy as jnp
from jax import lax
from jax.experimental import pallas as pl
from jax.experimental.pallas import tpu as pltpu
from jax.sharding import PartitionSpec as P

MESH = pl.DeviceIdType.MESH
PARTS = 4
TILES = 4
NT = (((1,), (1,)), ((), ()))
PARTNER, DIRECT, RELAYED, SECOND = 0, 1, 2, 3


def score(own, other, scale, bias, diagonal=False):
    logits = scale * lax.dot_general(own, other, NT, preferred_element_type=jnp.float32) + bias
    small = jnp.exp(-jnp.abs(logits))
    inverse = 1.0 / (1.0 + small)
    sigmoid = jnp.where(logits >= 0.0, inverse, small * inverse)
    signed = logits
    if diagonal:
        rows = lax.broadcasted_iota(jnp.int32, logits.shape, 0)
        match = lax.broadcasted_iota(jnp.int32, logits.shape, 1) == rows
        sigmoid = sigmoid - jnp.where(match, 1.0, 0.0)
        signed = jnp.where(match, -logits, logits)
    losses = jnp.maximum(signed, 0.0) + jnp.log1p(small)
    total = losses[:, 0:128]
    for first in range(128, losses.shape[1], 128):
        total += losses[:, first:first + 128]
    return total, (scale * sigmoid).astype(jnp.bfloat16)


def work(own, other, acc, loss, scale, bias):
    losses, coeff = score(own, other, scale, bias)
    acc[...] += jnp.dot(coeff, other, preferred_element_type=jnp.float32)
    loss[...] += losses


def ring_kernel(devices, image_ref, text_ref, scale_ref, bias_ref, acc, loss, own, second,
                blocks, load_sem, send, recv, here, ready):
    me = lax.axis_index("dp")
    core = lax.rem(me, 2)
    step = 2 * core - 1
    partner = me - step
    near = lax.rem(me + step + devices, devices)
    far = lax.rem(me + 2 * step + devices, devices)
    rows = own.shape[1]
    part = rows // PARTS

    barrier = pltpu.get_barrier_semaphore()
    previous = lax.rem(me - 1 - core + devices, devices)
    pl.semaphore_signal(barrier, inc=1, device_id=(previous,), device_id_type=MESH)

    @pl.when(core == 1)
    def _():
        pl.semaphore_signal(barrier, inc=1, device_id=(partner,), device_id_type=MESH)

    loads = [
        pltpu.make_async_copy(source, target, load_sem.at[slot])
        for slot, (source, target) in enumerate(((image_ref, own.at[0]), (text_ref, own.at[1])))
    ]

    def piece_of(index):
        return pl.ds(pl.multiple_of(index * part, part), part)

    def remote(source, way, index, device):
        target = second if way == SECOND else blocks.at[way]
        return pltpu.make_async_remote_copy(
            src_ref=source.at[piece_of(index)], dst_ref=target.at[piece_of(index)],
            send_sem=send.at[way, index], recv_sem=recv.at[way, index],
            device_id=(device,), device_id_type=MESH)

    def to_partner(source, index):
        return remote(source, PARTNER, index, partner)

    def to_far(source, index):
        return remote(source, DIRECT, index, far)

    def relay(index):
        return remote(blocks.at[DIRECT], RELAYED, index, partner)

    def to_near(index):
        return remote(blocks.at[PARTNER], SECOND, index, near)

    def each(action, first=0, last=PARTS):
        def run(index, carry):
            action(index)
            return carry
        lax.fori_loop(first, last, run, 0)

    @pl.when(core == 1)
    def _():
        pl.semaphore_wait(barrier, 2)
        each(lambda index: to_far(text_ref, index).start())
        pl.semaphore_wait(here, 1)
        pl.semaphore_signal(ready, inc=1, device_id=(near,), device_id_type=MESH)
        each(lambda index: to_partner(image_ref, index).start())
        for load in loads:
            load.start()

    @pl.when(core == 0)
    def _():
        pl.semaphore_wait(barrier, 1)
        pl.semaphore_signal(here, inc=1, device_id=(partner,), device_id_type=MESH)
        each(lambda index: to_partner(text_ref, index).start())
        for load in loads:
            load.start()
        pl.semaphore_wait(ready, 1)
        each(lambda index: to_far(image_ref, index).start())

    for load in loads:
        load.wait()
    scale = scale_ref[0]
    bias = bias_ref[0]

    for side in (0, 1):
        losses, coeff = score(own[side], own[1 - side], scale, bias, diagonal=True)
        acc[side] = jnp.dot(coeff, own[1 - side], preferred_element_type=jnp.float32)
        loss[side] = losses

    def visit(slot, carry):
        @pl.when(slot == PARTNER)
        def _():
            each(lambda index: to_partner(own.at[1 - core], index).wait_recv())

        @pl.when(slot == DIRECT)
        def _():
            each(lambda index: to_far(own.at[core], index).wait_send(), 0, PARTS - 1)
            to_near(0).start()
            to_far(own.at[core], PARTS - 1).wait_send()
            each(lambda index: to_near(index).start(), 1)

            def pass_on(index):
                to_far(own.at[core], index).wait_recv()
                relay(index).start()

            each(pass_on)

        @pl.when(slot == RELAYED)
        def _():
            each(lambda index: relay(index).wait_recv())

        side = jnp.where(slot == RELAYED, core, 1 - core)
        work(own[side], blocks[slot], acc.at[side], loss.at[side], scale, bias)
        return carry

    lax.fori_loop(PARTNER, SECOND, visit, 0)

    to_near(0).wait_recv()
    to_near(1).wait_recv()
    half = rows // 2
    work(own[core], second[0:half], acc.at[core], loss.at[core], scale, bias)
    to_near(2).wait_recv()
    work(own[core], second[half:half + part], acc.at[core], loss.at[core], scale, bias)

    def drain(index):
        to_partner(own.at[1 - core], index).wait_send()
        to_near(index).wait_send()
        relay(index).wait_send()

    each(drain)
    to_near(3).wait_recv()


def finish_kernel(acc, loss, own, second, scale_ref, bias_ref, loss_ref, image_ref, text_ref, row_loss, sems):
    core = lax.rem(lax.axis_index("dp"), 2)
    rows = loss.shape[1]
    tile = rows // TILES
    scale = scale_ref[0]
    bias = bias_ref[0]
    last = second[rows - rows // PARTS:]

    def store(side, target, slot, piece):
        return pltpu.make_async_copy(acc.at[side, piece], target.at[piece], sems.at[slot])

    whole = pl.ds(0, rows)

    def both(action):
        @pl.when(core == 1)
        def _():
            action(image_ref, text_ref)

        @pl.when(core == 0)
        def _():
            action(text_ref, image_ref)

    both(lambda done, open_: store(1 - core, done, TILES, whole).start())
    for index in range(TILES):
        piece = pl.ds(index * tile, tile)
        losses, coeff = score(own[core, piece], last, scale, bias)
        acc[core, piece] += jnp.dot(coeff, last, preferred_element_type=jnp.float32)
        loss[core, piece] += losses
        both(lambda done, open_: store(core, open_, index, piece).start())

    row_loss[...] = jnp.sum(loss[0].T, axis=0, keepdims=True) / (3.0 * rows)
    row_copy = pltpu.make_async_copy(row_loss, loss_ref, sems.at[TILES + 1])
    row_copy.start()
    store(1 - core, image_ref, TILES, whole).wait()
    for index in range(TILES):
        store(core, image_ref, index, pl.ds(index * tile, tile)).wait()
    row_copy.wait()


def body(image_embed, text_embed, logit_scale, logit_bias):
    rows, width = image_embed.shape
    devices = lax.axis_size("dp")
    anywhere = pl.BlockSpec(memory_space=pl.ANY)
    smem = pl.BlockSpec(memory_space=pltpu.SMEM)
    hbm = pl.BlockSpec(memory_space=pltpu.HBM)
    vmem = pl.BlockSpec(memory_space=pltpu.VMEM)
    images, texts = (pltpu.with_memory_space_constraint(a, pltpu.HBM) for a in (image_embed, text_embed))
    state = pl.pallas_call(
        functools.partial(ring_kernel, devices),
        out_shape=(
            pltpu.VMEM((2, rows, width), jnp.float32),
            pltpu.VMEM((2, rows, 128), jnp.float32),
            pltpu.VMEM((2, rows, width), jnp.bfloat16),
            pltpu.VMEM((rows, width), jnp.bfloat16),
        ),
        in_specs=[hbm, hbm, smem, smem],
        out_specs=(vmem, vmem, vmem, vmem),
        scratch_shapes=[
            pltpu.VMEM((3, rows, width), jnp.bfloat16),
            pltpu.SemaphoreType.DMA((2,)),
            pltpu.SemaphoreType.DMA((4, PARTS)),
            pltpu.SemaphoreType.DMA((4, PARTS)),
            pltpu.SemaphoreType.REGULAR,
            pltpu.SemaphoreType.REGULAR,
        ],
        compiler_params=pltpu.CompilerParams(
            collective_id=0, has_side_effects=True, vmem_limit_bytes=32 << 20),
        name="sigmoid_ring",
    )(images, texts, logit_scale, logit_bias)
    state = [pltpu.with_memory_space_constraint(a, pltpu.VMEM) for a in state]
    row_loss, grad_image, grad_text = pl.pallas_call(
        finish_kernel,
        out_shape=(
            jax.ShapeDtypeStruct((1, rows), jnp.float32),
            jax.ShapeDtypeStruct((rows, width), jnp.float32),
            jax.ShapeDtypeStruct((rows, width), jnp.float32),
        ),
        in_specs=[vmem, vmem, vmem, vmem, smem, smem],
        out_specs=(anywhere, anywhere, anywhere),
        scratch_shapes=[pltpu.VMEM((1, rows), jnp.float32), pltpu.SemaphoreType.DMA((TILES + 2,))],
        compiler_params=pltpu.CompilerParams(vmem_limit_bytes=8 << 20),
        name="finish",
    )(*state, logit_scale, logit_bias)
    return row_loss.reshape(rows), grad_image, grad_text


def solution(mesh):
    in_specs = (P("dp", None), P("dp", None), P(), P())
    out_specs = (P("dp"), P("dp", None), P("dp", None))
    return jax.shard_map(body, mesh=mesh, in_specs=in_specs, out_specs=out_specs, check_vma=False)
```

```python
import functools

import jax
import jax.numpy as jnp
from jax import lax
from jax.experimental import pallas as pl
from jax.experimental.pallas import tpu as pltpu
from jax.sharding import PartitionSpec as P

MESH = pl.DeviceIdType.MESH
PARTS = 4
TILES = 4
HEIGHT, DEPTH = 4, 16
NT = (((1,), (1,)), ((), ()))
PARTNER, DIRECT, RELAYED, SECOND = 0, 1, 2, 3


def score(own, other, scale, bias, diagonal=False):
    logits = scale * lax.dot_general(own, other, NT, preferred_element_type=jnp.float32) + bias
    small = jnp.exp(-jnp.abs(logits))
    inverse = 1.0 / (1.0 + small)
    sigmoid = jnp.where(logits >= 0.0, inverse, small * inverse)
    signed = logits
    if diagonal:
        rows = lax.broadcasted_iota(jnp.int32, logits.shape, 0)
        match = lax.broadcasted_iota(jnp.int32, logits.shape, 1) == rows
        sigmoid = sigmoid - jnp.where(match, 1.0, 0.0)
        signed = jnp.where(match, -logits, logits)
    losses = jnp.maximum(signed, 0.0) + jnp.log1p(small)
    total = losses[:, 0:128]
    for first in range(128, losses.shape[1], 128):
        total += losses[:, first:first + 128]
    return total, (scale * sigmoid).astype(jnp.bfloat16)


def work(own, other, acc, loss, scale, bias):
    losses, coeff = score(own, other, scale, bias)
    acc[...] += jnp.dot(coeff, other, preferred_element_type=jnp.float32)
    loss[...] += losses


def ring_kernel(devices, image_ref, text_ref, scale_ref, bias_ref, acc, loss, own, second,
                blocks, load_sem, send, recv, here, ready):
    me = lax.axis_index("dp")
    core = lax.rem(me, 2)
    step = 2 * core - 1
    partner = me - step
    near = lax.rem(me + step + devices, devices)
    far = lax.rem(me + 2 * step + devices, devices)
    rows = own.shape[1]
    part = rows // PARTS

    barrier = pltpu.get_barrier_semaphore()
    previous = lax.rem(me - 1 - core + devices, devices)
    pl.semaphore_signal(barrier, inc=1, device_id=(previous,), device_id_type=MESH)

    @pl.when(core == 1)
    def _():
        pl.semaphore_signal(barrier, inc=1, device_id=(partner,), device_id_type=MESH)

    loads = [
        pltpu.make_async_copy(source, target, load_sem.at[slot])
        for slot, (source, target) in enumerate(((image_ref, own.at[0]), (text_ref, own.at[1])))
    ]

    def piece_of(index):
        return pl.ds(pl.multiple_of(index * part, part), part)

    def remote(source, way, index, device):
        target = second if way == SECOND else blocks.at[way]
        return pltpu.make_async_remote_copy(
            src_ref=source.at[piece_of(index)], dst_ref=target.at[piece_of(index)],
            send_sem=send.at[way, index], recv_sem=recv.at[way, index],
            device_id=(device,), device_id_type=MESH)

    def to_partner(source, index):
        return remote(source, PARTNER, index, partner)

    def to_far(source, index):
        return remote(source, DIRECT, index, far)

    def relay(index):
        return remote(blocks.at[DIRECT], RELAYED, index, partner)

    def to_near(index):
        return remote(blocks.at[PARTNER], SECOND, index, near)

    def each(action, first=0, last=PARTS):
        def run(index, carry):
            action(index)
            return carry
        lax.fori_loop(first, last, run, 0)

    @pl.when(core == 1)
    def _():
        pl.semaphore_wait(barrier, 2)
        each(lambda index: to_far(text_ref, index).start())
        pl.semaphore_wait(here, 1)
        pl.semaphore_signal(ready, inc=1, device_id=(near,), device_id_type=MESH)
        each(lambda index: to_partner(image_ref, index).start())
        for load in loads:
            load.start()

    @pl.when(core == 0)
    def _():
        pl.semaphore_wait(barrier, 1)
        pl.semaphore_signal(here, inc=1, device_id=(partner,), device_id_type=MESH)
        each(lambda index: to_partner(text_ref, index).start())
        for load in loads:
            load.start()
        pl.semaphore_wait(ready, 1)
        each(lambda index: to_far(image_ref, index).start())

    for load in loads:
        load.wait()
    scale = scale_ref[0]
    bias = bias_ref[0]

    for side in (0, 1):
        losses, coeff = score(own[side], own[1 - side], scale, bias, diagonal=True)
        acc[side] = jnp.dot(coeff, own[1 - side], preferred_element_type=jnp.float32)
        loss[side] = losses

    def follow():
        each(lambda index: to_far(own.at[core], index).wait_send(), 0, PARTS - 1)
        to_near(0).start()
        to_far(own.at[core], PARTS - 1).wait_send()
        each(lambda index: to_near(index).start(), 1)

    def pass_on():
        def run(index):
            to_far(own.at[core], index).wait_recv()
            relay(index).start()
        each(run)

    chip = lax.div(me, 2)
    starts = lax.rem(chip, DEPTH) == 0
    corner = lax.rem(lax.div(chip, DEPTH), HEIGHT) == 0
    early_images = jnp.logical_and(starts, core == 0)
    late_texts = jnp.logical_and(starts, core == 1)

    def visit(phase, carry):
        slot = jnp.where(late_texts, jnp.where(phase == PARTNER, PARTNER, jnp.where(
            phase == 1, RELAYED, jnp.where((phase == 2) == corner, SECOND, DIRECT))), phase)

        @pl.when(slot == PARTNER)
        def _():
            each(lambda index: to_partner(own.at[1 - core], index).wait_recv())

        @pl.when(jnp.logical_and(slot == DIRECT, jnp.logical_not(early_images)))
        def _():
            pass_on()

        @pl.when(slot == RELAYED)
        def _():
            each(lambda index: relay(index).wait_recv())

        @pl.when(slot != SECOND)
        def _():
            side = jnp.where(slot == RELAYED, core, 1 - core)
            work(own[side], blocks[slot], acc.at[side], loss.at[side], scale, bias)

        @pl.when(slot == SECOND)
        def _():
            each(lambda index: to_near(index).wait_recv(), 0, PARTS - 1)
            work(own[core], second[0:rows - part], acc.at[core], loss.at[core], scale, bias)

        @pl.when(phase == 0)
        def _():
            @pl.when(early_images)
            def _():
                pass_on()

            follow()

        return carry

    lax.fori_loop(0, 4, visit, 0)

    def drain(index):
        to_partner(own.at[1 - core], index).wait_send()
        to_near(index).wait_send()
        relay(index).wait_send()

    each(drain)
    to_near(PARTS - 1).wait_recv()


def finish_kernel(acc, loss, own, second, scale_ref, bias_ref, loss_ref, image_ref, text_ref, row_loss, sems):
    core = lax.rem(lax.axis_index("dp"), 2)
    rows = loss.shape[1]
    tile = rows // TILES
    scale = scale_ref[0]
    bias = bias_ref[0]
    last = second[rows - rows // PARTS:]

    def store(side, target, slot, piece):
        return pltpu.make_async_copy(acc.at[side, piece], target.at[piece], sems.at[slot])

    whole = pl.ds(0, rows)

    def both(action):
        @pl.when(core == 1)
        def _():
            action(image_ref, text_ref)

        @pl.when(core == 0)
        def _():
            action(text_ref, image_ref)

    both(lambda done, open_: store(1 - core, done, TILES, whole).start())
    for index in range(TILES):
        piece = pl.ds(index * tile, tile)
        losses, coeff = score(own[core, piece], last, scale, bias)
        acc[core, piece] += jnp.dot(coeff, last, preferred_element_type=jnp.float32)
        loss[core, piece] += losses
        both(lambda done, open_: store(core, open_, index, piece).start())

    row_loss[...] = jnp.sum(loss[0].T, axis=0, keepdims=True) / (3.0 * rows)
    row_copy = pltpu.make_async_copy(row_loss, loss_ref, sems.at[TILES + 1])
    row_copy.start()
    store(1 - core, image_ref, TILES, whole).wait()
    for index in range(TILES):
        store(core, image_ref, index, pl.ds(index * tile, tile)).wait()
    row_copy.wait()


def body(image_embed, text_embed, logit_scale, logit_bias):
    rows, width = image_embed.shape
    devices = lax.axis_size("dp")
    anywhere = pl.BlockSpec(memory_space=pl.ANY)
    smem = pl.BlockSpec(memory_space=pltpu.SMEM)
    hbm = pl.BlockSpec(memory_space=pltpu.HBM)
    vmem = pl.BlockSpec(memory_space=pltpu.VMEM)
    images, texts = (pltpu.with_memory_space_constraint(a, pltpu.HBM) for a in (image_embed, text_embed))
    state = pl.pallas_call(
        functools.partial(ring_kernel, devices),
        out_shape=(
            pltpu.VMEM((2, rows, width), jnp.float32),
            pltpu.VMEM((2, rows, 128), jnp.float32),
            pltpu.VMEM((2, rows, width), jnp.bfloat16),
            pltpu.VMEM((rows, width), jnp.bfloat16),
        ),
        in_specs=[hbm, hbm, smem, smem],
        out_specs=(vmem, vmem, vmem, vmem),
        scratch_shapes=[
            pltpu.VMEM((3, rows, width), jnp.bfloat16),
            pltpu.SemaphoreType.DMA((2,)),
            pltpu.SemaphoreType.DMA((4, PARTS)),
            pltpu.SemaphoreType.DMA((4, PARTS)),
            pltpu.SemaphoreType.REGULAR,
            pltpu.SemaphoreType.REGULAR,
        ],
        compiler_params=pltpu.CompilerParams(
            collective_id=0, has_side_effects=True, vmem_limit_bytes=32 << 20),
        name="sigmoid_ring",
    )(images, texts, logit_scale, logit_bias)
    state = [pltpu.with_memory_space_constraint(a, pltpu.VMEM) for a in state]
    row_loss, grad_image, grad_text = pl.pallas_call(
        finish_kernel,
        out_shape=(
            jax.ShapeDtypeStruct((1, rows), jnp.float32),
            jax.ShapeDtypeStruct((rows, width), jnp.float32),
            jax.ShapeDtypeStruct((rows, width), jnp.float32),
        ),
        in_specs=[vmem, vmem, vmem, vmem, smem, smem],
        out_specs=(anywhere, anywhere, anywhere),
        scratch_shapes=[pltpu.VMEM((1, rows), jnp.float32), pltpu.SemaphoreType.DMA((TILES + 2,))],
        compiler_params=pltpu.CompilerParams(vmem_limit_bytes=8 << 20),
        name="finish",
    )(*state, logit_scale, logit_bias)
    return row_loss.reshape(rows), grad_image, grad_text


def solution(mesh):
    in_specs = (P("dp", None), P("dp", None), P(), P())
    out_specs = (P("dp"), P("dp", None), P("dp", None))
    return jax.shard_map(body, mesh=mesh, in_specs=in_specs, out_specs=out_specs, check_vma=False)
```

```python
import functools

import jax
import jax.numpy as jnp
from jax import lax
from jax.experimental import pallas as pl
from jax.experimental.pallas import tpu as pltpu
from jax.sharding import PartitionSpec as P

MESH = pl.DeviceIdType.MESH
PARTS = 4
TILES = 4
WIDTH, HEIGHT, DEPTH = 4, 4, 16
HELP = 32
NT = (((1,), (1,)), ((), ()))
PARTNER, DIRECT, RELAYED, SECOND = 0, 1, 2, 3


def score(own, other, scale, bias, diagonal=False):
    logits = scale * lax.dot_general(own, other, NT, preferred_element_type=jnp.float32) + bias
    small = jnp.exp(-jnp.abs(logits))
    inverse = 1.0 / (1.0 + small)
    sigmoid = jnp.where(logits >= 0.0, inverse, small * inverse)
    signed = logits
    if diagonal:
        rows = lax.broadcasted_iota(jnp.int32, logits.shape, 0)
        match = lax.broadcasted_iota(jnp.int32, logits.shape, 1) == rows
        sigmoid = sigmoid - jnp.where(match, 1.0, 0.0)
        signed = jnp.where(match, -logits, logits)
    losses = jnp.maximum(signed, 0.0) + jnp.log1p(small)
    total = losses[:, 0:128]
    for first in range(128, losses.shape[1], 128):
        total += losses[:, first:first + 128]
    return total, (scale * sigmoid).astype(jnp.bfloat16)


def work(own, other, acc, loss, scale, bias):
    losses, coeff = score(own, other, scale, bias)
    acc[...] += jnp.dot(coeff, other, preferred_element_type=jnp.float32)
    loss[...] += losses


def ring_kernel(devices, image_ref, text_ref, scale_ref, bias_ref, acc, loss, own, second,
                blocks, extra, load_sem, send, recv, here, helpers_in, help_ok,
                help_send, help_recv, lift_send, lift_recv):
    me = lax.axis_index("dp")
    core = lax.rem(me, 2)
    step = 2 * core - 1
    partner = me - step
    near = lax.rem(me + step + devices, devices)
    far = lax.rem(me + 2 * step + devices, devices)
    rows = own.shape[1]
    part = rows // PARTS

    chip = lax.div(me, 2)
    z = lax.rem(chip, DEPTH)
    y = lax.rem(lax.div(chip, DEPTH), HEIGHT)
    x = lax.div(chip, DEPTH * HEIGHT)
    starts = z == 0
    corner = y == 0

    barrier = pltpu.get_barrier_semaphore()

    def greet(distance):
        pl.semaphore_signal(
            barrier, inc=1, device_id=(lax.rem(me + distance + devices, devices),), device_id_type=MESH)

    greet(-1 - core)
    greet(2 - core)

    @pl.when(core == 1)
    def _():
        greet(-1)

    helpers = HEIGHT - 1
    ends = z == DEPTH - 1
    before = x != WIDTH - 1
    after = x != 0
    up_pole = jnp.logical_and(jnp.logical_and(ends, before), jnp.logical_and(y == helpers, core == 1))
    up_helper = jnp.logical_and(jnp.logical_and(ends, after), jnp.logical_and(y != helpers, core == 1))
    down_pole = jnp.logical_and(jnp.logical_and(starts, after), jnp.logical_and(corner, core == 0))
    down_helper = jnp.logical_and(jnp.logical_and(starts, before), jnp.logical_and(y != 0, core == 0))
    pole = jnp.logical_or(up_pole, down_pole)
    helper = jnp.logical_or(up_helper, down_helper)
    helper_line = y - 1 + core

    def device_at(x, y, z, core):
        return 2 * ((x * HEIGHT + y) * DEPTH + z) + core

    def up_helper_at(x, line):
        return device_at(x, line, DEPTH - 1, 1)

    def down_helper_at(x, line):
        return device_at(x, line + 1, 0, 0)

    up_pole_here = device_at(x, helpers, DEPTH - 1, 1)
    down_pole_here = device_at(x, 0, 0, 0)
    next_x = lax.rem(x + 1, WIDTH)
    last_x = lax.rem(x + WIDTH - 1, WIDTH)

    def tell(semaphore, device):
        pl.semaphore_signal(semaphore, inc=1, device_id=(device,), device_id_type=MESH)

    @pl.when(down_pole)
    def _():
        for line in range(helpers):
            tell(barrier, up_helper_at(x, line))

    @pl.when(down_helper)
    def _():
        tell(barrier, device_at(next_x, 0, 0, 0))

    def help_rows(line):
        return pl.ds(pl.multiple_of(rows - HELP * (helpers - line), HELP), HELP)

    def ask(line):
        device = jnp.where(core == 1, up_helper_at(next_x, line), down_helper_at(last_x, line))
        return pltpu.make_async_remote_copy(
            src_ref=blocks.at[PARTNER, help_rows(line)], dst_ref=extra, send_sem=help_send.at[line],
            recv_sem=help_recv, device_id=(device,), device_id_type=MESH)

    def lift(line):
        return pltpu.make_async_remote_copy(
            src_ref=extra, dst_ref=second.at[help_rows(line)], send_sem=lift_send, recv_sem=lift_recv.at[line],
            device_id=(jnp.where(core == 1, down_pole_here, up_pole_here),), device_id_type=MESH)

    def short():
        piece = pl.ds(rows - part, part - HELP * helpers)
        return pltpu.make_async_remote_copy(
            src_ref=blocks.at[PARTNER, piece], dst_ref=second.at[piece], send_sem=send.at[SECOND, PARTS - 1],
            recv_sem=recv.at[SECOND, PARTS - 1], device_id=(near,), device_id_type=MESH)

    loads = [
        pltpu.make_async_copy(source, target, load_sem.at[slot])
        for slot, (source, target) in enumerate(((image_ref, own.at[0]), (text_ref, own.at[1])))
    ]

    def piece_of(index):
        return pl.ds(pl.multiple_of(index * part, part), part)

    def remote(source, way, index, device):
        target = second if way == SECOND else blocks.at[way]
        return pltpu.make_async_remote_copy(
            src_ref=source.at[piece_of(index)], dst_ref=target.at[piece_of(index)],
            send_sem=send.at[way, index], recv_sem=recv.at[way, index],
            device_id=(device,), device_id_type=MESH)

    def to_partner(source, index):
        return remote(source, PARTNER, index, partner)

    def to_far(source, index):
        return remote(source, DIRECT, index, far)

    def relay(index):
        return remote(blocks.at[DIRECT], RELAYED, index, partner)

    def to_near(index):
        return remote(blocks.at[PARTNER], SECOND, index, near)

    def each(action, first=0, last=PARTS):
        def run(index, carry):
            action(index)
            return carry
        lax.fori_loop(first, last, run, 0)

    def start_zero():
        pl.semaphore_wait(barrier, jnp.where(down_pole, 3 + helpers, 3))
        pl.semaphore_signal(here, inc=1, device_id=(partner,), device_id_type=MESH)
        each(lambda index: to_far(image_ref, index).start())
        each(lambda index: to_partner(text_ref, index).start())

        @pl.when(down_pole)
        def _():
            for line in range(helpers):
                tell(help_ok, down_helper_at(last_x, line))
            pl.semaphore_wait(helpers_in, helpers)
            tell(help_ok, lax.rem(me - 1 + devices, devices))

    def start_one():
        pl.semaphore_wait(here, 1)
        each(lambda index: to_partner(image_ref, index).start())

    def when(core_is, starts_is, action):
        @pl.when(jnp.logical_and(core == core_is, starts if starts_is else jnp.logical_not(starts)))
        def _():
            action()

    @pl.when(core == 1)
    def _():
        pl.semaphore_wait(barrier, jnp.where(up_helper, 3, 2))
        each(lambda index: to_far(text_ref, index).start())

        @pl.when(up_helper)
        def _():
            tell(helpers_in, down_pole_here)

    for load in loads:
        load.start()

    when(0, False, start_zero)
    when(1, False, start_one)
    for load in loads:
        load.wait()
    scale = scale_ref[0]
    bias = bias_ref[0]

    for side in (0, 1):
        losses, coeff = score(own[side], own[1 - side], scale, bias, diagonal=True)
        acc[side] = jnp.dot(coeff, own[1 - side], preferred_element_type=jnp.float32)
        loss[side] = losses

    def follow():
        each(lambda index: to_far(own.at[core], index).wait_send(), 0, PARTS - 1)

        @pl.when(up_pole)
        def _():
            pl.semaphore_wait(help_ok, 1)

        @pl.when(pole)
        def _():
            for line in range(helpers):
                ask(line).start()

        to_near(0).start()
        to_far(own.at[core], PARTS - 1).wait_send()
        each(lambda index: to_near(index).start(), 1, PARTS - 1)

        @pl.when(pole)
        def _():
            short().start()

        @pl.when(jnp.logical_not(jnp.logical_or(pole, up_helper)))
        def _():
            to_near(PARTS - 1).start()

    def carry_over():
        ask(helper_line).wait_recv()
        lift(helper_line).start()

    def pass_on(first=0, last=PARTS):
        def run(index):
            to_far(own.at[core], index).wait_recv()
            relay(index).start()
        each(run, first, last)

    early_images = jnp.logical_and(starts, core == 0)
    late_texts = jnp.logical_and(starts, core == 1)
    late_corner = jnp.logical_and(late_texts, corner)

    when(0, True, start_zero)
    when(1, True, start_one)

    def visit(phase, carry):
        @pl.when(jnp.logical_and(up_helper, phase == 1))
        def _():
            carry_over()
            to_near(PARTS - 1).start()

        @pl.when(jnp.logical_and(down_helper, phase == 2))
        def _():
            pl.semaphore_wait(help_ok, 1)
            carry_over()

        slot = jnp.where(late_texts, jnp.where(phase == PARTNER, PARTNER, jnp.where(
            phase == 1, RELAYED, jnp.where((phase == 2) == corner, SECOND, DIRECT))), phase)

        @pl.when(slot == PARTNER)
        def _():
            each(lambda index: to_partner(own.at[1 - core], index).wait_recv())

        @pl.when(jnp.logical_and(slot == DIRECT, jnp.logical_not(early_images)))
        def _():
            pass_on(jnp.where(late_corner, PARTS // 2, 0))

        @pl.when(slot == RELAYED)
        def _():
            each(lambda index: relay(index).wait_recv())

        @pl.when(slot != SECOND)
        def _():
            side = jnp.where(slot == RELAYED, core, 1 - core)
            work(own[side], blocks[slot], acc.at[side], loss.at[side], scale, bias)

        @pl.when(slot == SECOND)
        def _():
            @pl.when(late_corner)
            def _():
                pass_on(0, PARTS // 2)

            each(lambda index: to_near(index).wait_recv(), 0, PARTS - 1)
            work(own[core], second[0:rows - part], acc.at[core], loss.at[core], scale, bias)

        @pl.when(phase == 0)
        def _():
            @pl.when(early_images)
            def _():
                pass_on()

            follow()

        return carry

    lax.fori_loop(0, 4, visit, 0)

    def drain(index):
        to_partner(own.at[1 - core], index).wait_send()
        relay(index).wait_send()

    each(drain)
    each(lambda index: to_near(index).wait_send(), 0, PARTS - 1)

    @pl.when(pole)
    def _():
        short().wait_send()
        for line in range(helpers):
            ask(line).wait_send()

    @pl.when(jnp.logical_not(pole))
    def _():
        to_near(PARTS - 1).wait_send()

    @pl.when(helper)
    def _():
        lift(helper_line).wait_send()

    @pl.when(pole)
    def _():
        for line in range(helpers):
            lift(line).wait_recv()
        short().wait_recv()

    @pl.when(jnp.logical_not(pole))
    def _():
        to_near(PARTS - 1).wait_recv()


def finish_kernel(acc, loss, own, second, scale_ref, bias_ref, loss_ref, image_ref, text_ref, row_loss, sems):
    core = lax.rem(lax.axis_index("dp"), 2)
    rows = loss.shape[1]
    tile = rows // TILES
    scale = scale_ref[0]
    bias = bias_ref[0]
    last = second[rows - rows // PARTS:]

    def store(side, target, slot, piece):
        return pltpu.make_async_copy(acc.at[side, piece], target.at[piece], sems.at[slot])

    whole = pl.ds(0, rows)

    def both(action):
        @pl.when(core == 1)
        def _():
            action(image_ref, text_ref)

        @pl.when(core == 0)
        def _():
            action(text_ref, image_ref)

    both(lambda done, open_: store(1 - core, done, TILES, whole).start())
    for index in range(TILES):
        piece = pl.ds(index * tile, tile)
        losses, coeff = score(own[core, piece], last, scale, bias)
        acc[core, piece] += jnp.dot(coeff, last, preferred_element_type=jnp.float32)
        loss[core, piece] += losses
        both(lambda done, open_: store(core, open_, index, piece).start())

    row_loss[...] = jnp.sum(loss[0].T, axis=0, keepdims=True) / (3.0 * rows)
    row_copy = pltpu.make_async_copy(row_loss, loss_ref, sems.at[TILES + 1])
    row_copy.start()
    store(1 - core, image_ref, TILES, whole).wait()
    for index in range(TILES):
        store(core, image_ref, index, pl.ds(index * tile, tile)).wait()
    row_copy.wait()


def body(image_embed, text_embed, logit_scale, logit_bias):
    rows, width = image_embed.shape
    devices = lax.axis_size("dp")
    anywhere = pl.BlockSpec(memory_space=pl.ANY)
    smem = pl.BlockSpec(memory_space=pltpu.SMEM)
    hbm = pl.BlockSpec(memory_space=pltpu.HBM)
    vmem = pl.BlockSpec(memory_space=pltpu.VMEM)
    images, texts = (pltpu.with_memory_space_constraint(a, pltpu.HBM) for a in (image_embed, text_embed))
    state = pl.pallas_call(
        functools.partial(ring_kernel, devices),
        out_shape=(
            pltpu.VMEM((2, rows, width), jnp.float32),
            pltpu.VMEM((2, rows, 128), jnp.float32),
            pltpu.VMEM((2, rows, width), jnp.bfloat16),
            pltpu.VMEM((rows, width), jnp.bfloat16),
        ),
        in_specs=[hbm, hbm, smem, smem],
        out_specs=(vmem, vmem, vmem, vmem),
        scratch_shapes=[
            pltpu.VMEM((3, rows, width), jnp.bfloat16),
            pltpu.VMEM((HELP, width), jnp.bfloat16),
            pltpu.SemaphoreType.DMA((2,)),
            pltpu.SemaphoreType.DMA((4, PARTS)),
            pltpu.SemaphoreType.DMA((4, PARTS)),
            pltpu.SemaphoreType.REGULAR,
            pltpu.SemaphoreType.REGULAR,
            pltpu.SemaphoreType.REGULAR,
            pltpu.SemaphoreType.DMA((HEIGHT - 1,)),
            pltpu.SemaphoreType.DMA,
            pltpu.SemaphoreType.DMA,
            pltpu.SemaphoreType.DMA((HEIGHT - 1,)),
        ],
        compiler_params=pltpu.CompilerParams(
            collective_id=0, has_side_effects=True, vmem_limit_bytes=32 << 20),
        name="sigmoid_ring",
    )(images, texts, logit_scale, logit_bias)
    state = [pltpu.with_memory_space_constraint(a, pltpu.VMEM) for a in state]
    row_loss, grad_image, grad_text = pl.pallas_call(
        finish_kernel,
        out_shape=(
            jax.ShapeDtypeStruct((1, rows), jnp.float32),
            jax.ShapeDtypeStruct((rows, width), jnp.float32),
            jax.ShapeDtypeStruct((rows, width), jnp.float32),
        ),
        in_specs=[vmem, vmem, vmem, vmem, smem, smem],
        out_specs=(anywhere, anywhere, anywhere),
        scratch_shapes=[pltpu.VMEM((1, rows), jnp.float32), pltpu.SemaphoreType.DMA((TILES + 2,))],
        compiler_params=pltpu.CompilerParams(vmem_limit_bytes=8 << 20),
        name="finish",
    )(*state, logit_scale, logit_bias)
    return row_loss.reshape(rows), grad_image, grad_text


def solution(mesh):
    in_specs = (P("dp", None), P("dp", None), P(), P())
    out_specs = (P("dp"), P("dp", None), P("dp", None))
    return jax.shard_map(body, mesh=mesh, in_specs=in_specs, out_specs=out_specs, check_vma=False)
```

```python
import functools

import jax
import jax.numpy as jnp
from jax import lax
from jax.experimental import pallas as pl
from jax.experimental.pallas import tpu as pltpu
from jax.sharding import PartitionSpec as P

MESH = pl.DeviceIdType.MESH
PARTS = 4
TILES = 4
WIDTH, HEIGHT, DEPTH = 4, 4, 16
HELP = (48, 32, 16)
NT = (((1,), (1,)), ((), ()))
PARTNER, DIRECT, RELAYED, SECOND = 0, 1, 2, 3


def score(own, other, scale, bias, diagonal=False):
    logits = scale * lax.dot_general(own, other, NT, preferred_element_type=jnp.float32) + bias
    small = jnp.exp(-jnp.abs(logits))
    inverse = 1.0 / (1.0 + small)
    sigmoid = jnp.where(logits >= 0.0, inverse, small * inverse)
    signed = logits
    if diagonal:
        rows = lax.broadcasted_iota(jnp.int32, logits.shape, 0)
        match = lax.broadcasted_iota(jnp.int32, logits.shape, 1) == rows
        sigmoid = sigmoid - jnp.where(match, 1.0, 0.0)
        signed = jnp.where(match, -logits, logits)
    losses = jnp.maximum(signed, 0.0) + jnp.log1p(small)
    total = losses[:, 0:128]
    for first in range(128, losses.shape[1], 128):
        total += losses[:, first:first + 128]
    return total, (scale * sigmoid).astype(jnp.bfloat16)


def work(own, other, acc, loss, scale, bias):
    losses, coeff = score(own, other, scale, bias)
    acc[...] += jnp.dot(coeff, other, preferred_element_type=jnp.float32)
    loss[...] += losses


def ring_kernel(devices, image_ref, text_ref, scale_ref, bias_ref, acc, loss, own, second,
                blocks, extra, load_sem, send, recv, here, helpers_in, help_ok,
                help_send, help_recv, lift_send, lift_recv):
    me = lax.axis_index("dp")
    core = lax.rem(me, 2)
    step = 2 * core - 1
    partner = me - step
    near = lax.rem(me + step + devices, devices)
    far = lax.rem(me + 2 * step + devices, devices)
    rows = own.shape[1]
    part = rows // PARTS

    chip = lax.div(me, 2)
    z = lax.rem(chip, DEPTH)
    y = lax.rem(lax.div(chip, DEPTH), HEIGHT)
    x = lax.div(chip, DEPTH * HEIGHT)
    starts = z == 0
    corner = y == 0

    barrier = pltpu.get_barrier_semaphore()

    def greet(distance):
        pl.semaphore_signal(
            barrier, inc=1, device_id=(lax.rem(me + distance + devices, devices),), device_id_type=MESH)

    greet(-1 - core)
    greet(2 - core)

    @pl.when(core == 1)
    def _():
        greet(-1)

    helpers = HEIGHT - 1
    ends = z == DEPTH - 1
    before = x != WIDTH - 1
    after = x != 0
    up_pole = jnp.logical_and(jnp.logical_and(ends, before), jnp.logical_and(y == helpers, core == 1))
    up_helper = jnp.logical_and(jnp.logical_and(ends, after), jnp.logical_and(y != helpers, core == 1))
    down_pole = jnp.logical_and(jnp.logical_and(starts, after), jnp.logical_and(corner, core == 0))
    down_helper = jnp.logical_and(jnp.logical_and(starts, before), jnp.logical_and(y != 0, core == 0))
    pole = jnp.logical_or(up_pole, down_pole)
    helper = jnp.logical_or(up_helper, down_helper)
    helper_line = y - 1 + core

    def device_at(x, y, z, core):
        return 2 * ((x * HEIGHT + y) * DEPTH + z) + core

    def up_helper_at(x, line):
        return device_at(x, line, DEPTH - 1, 1)

    def down_helper_at(x, line):
        return device_at(x, line + 1, 0, 0)

    up_pole_here = device_at(x, helpers, DEPTH - 1, 1)
    down_pole_here = device_at(x, 0, 0, 0)
    next_x = lax.rem(x + 1, WIDTH)
    last_x = lax.rem(x + WIDTH - 1, WIDTH)

    def tell(semaphore, device):
        pl.semaphore_signal(semaphore, inc=1, device_id=(device,), device_id_type=MESH)

    @pl.when(down_pole)
    def _():
        for line in range(helpers):
            tell(barrier, up_helper_at(x, line))

    @pl.when(down_helper)
    def _():
        tell(barrier, device_at(next_x, 0, 0, 0))

    def help_rows(line):
        return pl.ds(rows - sum(HELP[line:]), HELP[line])

    def ask(line):
        device = jnp.where(core == 1, up_helper_at(next_x, line), down_helper_at(last_x, line))
        return pltpu.make_async_remote_copy(
            src_ref=blocks.at[PARTNER, help_rows(line)], dst_ref=extra.at[pl.ds(0, HELP[line])],
            send_sem=help_send.at[line], recv_sem=help_recv, device_id=(device,), device_id_type=MESH)

    def lift(line):
        return pltpu.make_async_remote_copy(
            src_ref=extra.at[pl.ds(0, HELP[line])], dst_ref=second.at[help_rows(line)], send_sem=lift_send,
            recv_sem=lift_recv.at[line], device_id=(jnp.where(core == 1, down_pole_here, up_pole_here),),
            device_id_type=MESH)

    def on_line(action):
        for line in range(helpers):
            @pl.when(helper_line == line)
            def _():
                action(line)

    def short():
        piece = pl.ds(rows - part, part - sum(HELP))
        return pltpu.make_async_remote_copy(
            src_ref=blocks.at[PARTNER, piece], dst_ref=second.at[piece], send_sem=send.at[SECOND, PARTS - 1],
            recv_sem=recv.at[SECOND, PARTS - 1], device_id=(near,), device_id_type=MESH)

    loads = [
        pltpu.make_async_copy(source, target, load_sem.at[slot])
        for slot, (source, target) in enumerate(((image_ref, own.at[0]), (text_ref, own.at[1])))
    ]

    def piece_of(index):
        return pl.ds(pl.multiple_of(index * part, part), part)

    def remote(source, way, index, device):
        target = second if way == SECOND else blocks.at[way]
        return pltpu.make_async_remote_copy(
            src_ref=source.at[piece_of(index)], dst_ref=target.at[piece_of(index)],
            send_sem=send.at[way, index], recv_sem=recv.at[way, index],
            device_id=(device,), device_id_type=MESH)

    def to_partner(source, index):
        return remote(source, PARTNER, index, partner)

    def to_far(source, index):
        return remote(source, DIRECT, index, far)

    def relay(index):
        return remote(blocks.at[DIRECT], RELAYED, index, partner)

    def to_near(index):
        return remote(blocks.at[PARTNER], SECOND, index, near)

    def each(action, first=0, last=PARTS):
        def run(index, carry):
            action(index)
            return carry
        lax.fori_loop(first, last, run, 0)

    def start_zero():
        pl.semaphore_wait(barrier, jnp.where(down_pole, 3 + helpers, 3))
        pl.semaphore_signal(here, inc=1, device_id=(partner,), device_id_type=MESH)
        each(lambda index: to_far(image_ref, index).start())
        each(lambda index: to_partner(text_ref, index).start())

        @pl.when(down_pole)
        def _():
            for line in range(helpers):
                tell(help_ok, down_helper_at(last_x, line))
            pl.semaphore_wait(helpers_in, helpers)
            tell(help_ok, lax.rem(me - 1 + devices, devices))

    def start_one():
        pl.semaphore_wait(here, 1)
        each(lambda index: to_partner(image_ref, index).start())

    def when(core_is, starts_is, action):
        @pl.when(jnp.logical_and(core == core_is, starts if starts_is else jnp.logical_not(starts)))
        def _():
            action()

    @pl.when(core == 1)
    def _():
        pl.semaphore_wait(barrier, jnp.where(up_helper, 3, 2))
        each(lambda index: to_far(text_ref, index).start())

        @pl.when(up_helper)
        def _():
            tell(helpers_in, down_pole_here)

    for load in loads:
        load.start()

    when(0, False, start_zero)
    when(1, False, start_one)
    for load in loads:
        load.wait()
    scale = scale_ref[0]
    bias = bias_ref[0]

    for side in (0, 1):
        losses, coeff = score(own[side], own[1 - side], scale, bias, diagonal=True)
        acc[side] = jnp.dot(coeff, own[1 - side], preferred_element_type=jnp.float32)
        loss[side] = losses

    def follow():
        each(lambda index: to_far(own.at[core], index).wait_send(), 0, PARTS - 1)

        @pl.when(up_pole)
        def _():
            pl.semaphore_wait(help_ok, 1)

        @pl.when(pole)
        def _():
            for line in range(helpers):
                ask(line).start()

        to_near(0).start()
        to_far(own.at[core], PARTS - 1).wait_send()
        each(lambda index: to_near(index).start(), 1, PARTS - 1)

        @pl.when(pole)
        def _():
            short().start()

        @pl.when(jnp.logical_not(jnp.logical_or(pole, up_helper)))
        def _():
            to_near(PARTS - 1).start()

    def carry_over():
        def run(line):
            ask(line).wait_recv()
            lift(line).start()

        on_line(run)

    def pass_on(first=0, last=PARTS):
        def run(index):
            to_far(own.at[core], index).wait_recv()
            relay(index).start()
        each(run, first, last)

    early_images = jnp.logical_and(starts, core == 0)
    late_texts = jnp.logical_and(starts, core == 1)
    late_corner = jnp.logical_and(late_texts, corner)

    when(0, True, start_zero)
    when(1, True, start_one)

    def visit(phase, carry):
        @pl.when(jnp.logical_and(up_helper, phase == 1))
        def _():
            carry_over()
            to_near(PARTS - 1).start()

        @pl.when(jnp.logical_and(down_helper, phase == 3))
        def _():
            pl.semaphore_wait(help_ok, 1)
            carry_over()

        slot = jnp.where(late_texts, jnp.where(phase == PARTNER, PARTNER, jnp.where(
            phase == 1, RELAYED, jnp.where((phase == 2) == corner, SECOND, DIRECT))), phase)

        @pl.when(slot == PARTNER)
        def _():
            each(lambda index: to_partner(own.at[1 - core], index).wait_recv())

        @pl.when(jnp.logical_and(slot == DIRECT, jnp.logical_not(early_images)))
        def _():
            pass_on(jnp.where(late_corner, PARTS // 2, 0))

        @pl.when(slot == RELAYED)
        def _():
            each(lambda index: relay(index).wait_recv())

        @pl.when(slot != SECOND)
        def _():
            side = jnp.where(slot == RELAYED, core, 1 - core)
            work(own[side], blocks[slot], acc.at[side], loss.at[side], scale, bias)

        @pl.when(slot == SECOND)
        def _():
            @pl.when(late_corner)
            def _():
                pass_on(0, PARTS // 2)

            half = rows // 2
            each(lambda index: to_near(index).wait_recv(), 0, PARTS // 2)
            work(own[core], second[0:half], acc.at[core], loss.at[core], scale, bias)
            to_near(PARTS // 2).wait_recv()
            work(own[core], second[half:half + part], acc.at[core], loss.at[core], scale, bias)

        @pl.when(phase == 0)
        def _():
            @pl.when(early_images)
            def _():
                pass_on()

            follow()

        return carry

    lax.fori_loop(0, 4, visit, 0)

    def drain(index):
        to_partner(own.at[1 - core], index).wait_send()
        relay(index).wait_send()

    each(drain)
    each(lambda index: to_near(index).wait_send(), 0, PARTS - 1)

    @pl.when(pole)
    def _():
        short().wait_send()
        for line in range(helpers):
            ask(line).wait_send()

    @pl.when(jnp.logical_not(pole))
    def _():
        to_near(PARTS - 1).wait_send()

    @pl.when(helper)
    def _():
        on_line(lambda line: lift(line).wait_send())

    @pl.when(pole)
    def _():
        for line in range(helpers):
            lift(line).wait_recv()
        short().wait_recv()

    @pl.when(jnp.logical_not(pole))
    def _():
        to_near(PARTS - 1).wait_recv()


def finish_kernel(acc, loss, own, second, scale_ref, bias_ref, loss_ref, image_ref, text_ref, row_loss, sems):
    core = lax.rem(lax.axis_index("dp"), 2)
    rows = loss.shape[1]
    tile = rows // TILES
    scale = scale_ref[0]
    bias = bias_ref[0]
    last = second[rows - rows // PARTS:]

    def store(side, target, slot, piece):
        return pltpu.make_async_copy(acc.at[side, piece], target.at[piece], sems.at[slot])

    whole = pl.ds(0, rows)

    def both(action):
        @pl.when(core == 1)
        def _():
            action(image_ref, text_ref)

        @pl.when(core == 0)
        def _():
            action(text_ref, image_ref)

    both(lambda done, open_: store(1 - core, done, TILES, whole).start())
    for index in range(TILES):
        piece = pl.ds(index * tile, tile)
        losses, coeff = score(own[core, piece], last, scale, bias)
        acc[core, piece] += jnp.dot(coeff, last, preferred_element_type=jnp.float32)
        loss[core, piece] += losses
        both(lambda done, open_: store(core, open_, index, piece).start())

    row_loss[...] = jnp.sum(loss[0].T, axis=0, keepdims=True) / (3.0 * rows)
    row_copy = pltpu.make_async_copy(row_loss, loss_ref, sems.at[TILES + 1])
    row_copy.start()
    store(1 - core, image_ref, TILES, whole).wait()
    for index in range(TILES):
        store(core, image_ref, index, pl.ds(index * tile, tile)).wait()
    row_copy.wait()


def body(image_embed, text_embed, logit_scale, logit_bias):
    rows, width = image_embed.shape
    devices = lax.axis_size("dp")
    anywhere = pl.BlockSpec(memory_space=pl.ANY)
    smem = pl.BlockSpec(memory_space=pltpu.SMEM)
    hbm = pl.BlockSpec(memory_space=pltpu.HBM)
    vmem = pl.BlockSpec(memory_space=pltpu.VMEM)
    images, texts = (pltpu.with_memory_space_constraint(a, pltpu.HBM) for a in (image_embed, text_embed))
    state = pl.pallas_call(
        functools.partial(ring_kernel, devices),
        out_shape=(
            pltpu.VMEM((2, rows, width), jnp.float32),
            pltpu.VMEM((2, rows, 128), jnp.float32),
            pltpu.VMEM((2, rows, width), jnp.bfloat16),
            pltpu.VMEM((rows, width), jnp.bfloat16),
        ),
        in_specs=[hbm, hbm, smem, smem],
        out_specs=(vmem, vmem, vmem, vmem),
        scratch_shapes=[
            pltpu.VMEM((3, rows, width), jnp.bfloat16),
            pltpu.VMEM((max(HELP), width), jnp.bfloat16),
            pltpu.SemaphoreType.DMA((2,)),
            pltpu.SemaphoreType.DMA((4, PARTS)),
            pltpu.SemaphoreType.DMA((4, PARTS)),
            pltpu.SemaphoreType.REGULAR,
            pltpu.SemaphoreType.REGULAR,
            pltpu.SemaphoreType.REGULAR,
            pltpu.SemaphoreType.DMA((HEIGHT - 1,)),
            pltpu.SemaphoreType.DMA,
            pltpu.SemaphoreType.DMA,
            pltpu.SemaphoreType.DMA((HEIGHT - 1,)),
        ],
        compiler_params=pltpu.CompilerParams(
            collective_id=0, has_side_effects=True, vmem_limit_bytes=32 << 20),
        name="sigmoid_ring",
    )(images, texts, logit_scale, logit_bias)
    state = [pltpu.with_memory_space_constraint(a, pltpu.VMEM) for a in state]
    row_loss, grad_image, grad_text = pl.pallas_call(
        finish_kernel,
        out_shape=(
            jax.ShapeDtypeStruct((1, rows), jnp.float32),
            jax.ShapeDtypeStruct((rows, width), jnp.float32),
            jax.ShapeDtypeStruct((rows, width), jnp.float32),
        ),
        in_specs=[vmem, vmem, vmem, vmem, smem, smem],
        out_specs=(anywhere, anywhere, anywhere),
        scratch_shapes=[pltpu.VMEM((1, rows), jnp.float32), pltpu.SemaphoreType.DMA((TILES + 2,))],
        compiler_params=pltpu.CompilerParams(vmem_limit_bytes=8 << 20),
        name="finish",
    )(*state, logit_scale, logit_bias)
    return row_loss.reshape(rows), grad_image, grad_text


def solution(mesh):
    in_specs = (P("dp", None), P("dp", None), P(), P())
    out_specs = (P("dp"), P("dp", None), P("dp", None))
    return jax.shard_map(body, mesh=mesh, in_specs=in_specs, out_specs=out_specs, check_vma=False)
```

```python
import functools

import jax
import jax.numpy as jnp
from jax import lax
from jax.experimental import pallas as pl
from jax.experimental.pallas import tpu as pltpu
from jax.sharding import PartitionSpec as P

MESH = pl.DeviceIdType.MESH
PARTS = 4
TILES = 4
WIDTH, HEIGHT, DEPTH = 4, 4, 16
HELP = (48, 32, 16)
NT = (((1,), (1,)), ((), ()))
PARTNER, DIRECT, RELAYED, SECOND = 0, 1, 2, 3


def score(own, other, scale, bias, diagonal=False):
    logits = scale * lax.dot_general(own, other, NT, preferred_element_type=jnp.float32) + bias
    small = jnp.exp(-jnp.abs(logits))
    inverse = 1.0 / (1.0 + small)
    sigmoid = jnp.where(logits >= 0.0, inverse, small * inverse)
    signed = logits
    if diagonal:
        rows = lax.broadcasted_iota(jnp.int32, logits.shape, 0)
        match = lax.broadcasted_iota(jnp.int32, logits.shape, 1) == rows
        sigmoid = sigmoid - jnp.where(match, 1.0, 0.0)
        signed = jnp.where(match, -logits, logits)
    losses = jnp.maximum(signed, 0.0) + jnp.log1p(small)
    total = losses[:, 0:128]
    for first in range(128, losses.shape[1], 128):
        total += losses[:, first:first + 128]
    return total, (scale * sigmoid).astype(jnp.bfloat16)


def work(own, other, acc, loss, scale, bias):
    losses, coeff = score(own, other, scale, bias)
    acc[...] += jnp.dot(coeff, other, preferred_element_type=jnp.float32)
    loss[...] += losses


def ring_kernel(devices, image_ref, text_ref, scale_ref, bias_ref, acc, loss, own, second,
                blocks, extra, load_sem, send, recv, here, helpers_in, help_ok,
                help_send, help_recv, lift_send, lift_recv):
    me = lax.axis_index("dp")
    core = lax.rem(me, 2)
    step = 2 * core - 1
    partner = me - step
    near = lax.rem(me + step + devices, devices)
    far = lax.rem(me + 2 * step + devices, devices)
    rows = own.shape[1]
    part = rows // PARTS

    chip = lax.div(me, 2)
    z = lax.rem(chip, DEPTH)
    y = lax.rem(lax.div(chip, DEPTH), HEIGHT)
    x = lax.div(chip, DEPTH * HEIGHT)
    starts = z == 0
    corner = y == 0

    barrier = pltpu.get_barrier_semaphore()

    def greet(distance):
        pl.semaphore_signal(
            barrier, inc=1, device_id=(lax.rem(me + distance + devices, devices),), device_id_type=MESH)

    greet(2 - core)
    greet(-1 - core)

    @pl.when(core == 1)
    def _():
        greet(-1)

    helpers = HEIGHT - 1
    ends = z == DEPTH - 1
    before = x != WIDTH - 1
    after = x != 0
    up_pole = jnp.logical_and(jnp.logical_and(ends, before), jnp.logical_and(y == helpers, core == 1))
    up_helper = jnp.logical_and(jnp.logical_and(ends, after), jnp.logical_and(y != helpers, core == 1))
    down_pole = jnp.logical_and(jnp.logical_and(starts, after), jnp.logical_and(corner, core == 0))
    down_helper = jnp.logical_and(jnp.logical_and(starts, before), jnp.logical_and(y != 0, core == 0))
    pole = jnp.logical_or(up_pole, down_pole)
    helper = jnp.logical_or(up_helper, down_helper)
    helper_line = y - 1 + core

    def device_at(x, y, z, core):
        return 2 * ((x * HEIGHT + y) * DEPTH + z) + core

    def up_helper_at(x, line):
        return device_at(x, line, DEPTH - 1, 1)

    def down_helper_at(x, line):
        return device_at(x, line + 1, 0, 0)

    up_pole_here = device_at(x, helpers, DEPTH - 1, 1)
    down_pole_here = device_at(x, 0, 0, 0)
    next_x = lax.rem(x + 1, WIDTH)
    last_x = lax.rem(x + WIDTH - 1, WIDTH)

    def tell(semaphore, device):
        pl.semaphore_signal(semaphore, inc=1, device_id=(device,), device_id_type=MESH)

    @pl.when(down_pole)
    def _():
        for line in range(helpers):
            tell(barrier, up_helper_at(x, line))

    @pl.when(down_helper)
    def _():
        tell(barrier, device_at(next_x, 0, 0, 0))

    def help_rows(line):
        return pl.ds(rows - sum(HELP[line:]), HELP[line])

    def ask(line):
        device = jnp.where(core == 1, up_helper_at(next_x, line), down_helper_at(last_x, line))
        return pltpu.make_async_remote_copy(
            src_ref=blocks.at[PARTNER, help_rows(line)], dst_ref=extra.at[pl.ds(0, HELP[line])],
            send_sem=help_send.at[line], recv_sem=help_recv, device_id=(device,), device_id_type=MESH)

    def lift(line):
        return pltpu.make_async_remote_copy(
            src_ref=extra.at[pl.ds(0, HELP[line])], dst_ref=second.at[help_rows(line)], send_sem=lift_send,
            recv_sem=lift_recv.at[line], device_id=(jnp.where(core == 1, down_pole_here, up_pole_here),),
            device_id_type=MESH)

    def on_line(action):
        for line in range(helpers):
            @pl.when(helper_line == line)
            def _():
                action(line)

    def short():
        piece = pl.ds(rows - part, part - sum(HELP))
        return pltpu.make_async_remote_copy(
            src_ref=blocks.at[PARTNER, piece], dst_ref=second.at[piece], send_sem=send.at[SECOND, PARTS - 1],
            recv_sem=recv.at[SECOND, PARTS - 1], device_id=(near,), device_id_type=MESH)

    loads = [
        pltpu.make_async_copy(source, target, load_sem.at[slot])
        for slot, (source, target) in enumerate(((image_ref, own.at[0]), (text_ref, own.at[1])))
    ]

    def piece_of(index):
        return pl.ds(pl.multiple_of(index * part, part), part)

    def remote(source, way, index, device):
        target = second if way == SECOND else blocks.at[way]
        return pltpu.make_async_remote_copy(
            src_ref=source.at[piece_of(index)], dst_ref=target.at[piece_of(index)],
            send_sem=send.at[way, index], recv_sem=recv.at[way, index],
            device_id=(device,), device_id_type=MESH)

    def to_partner(source, index):
        return remote(source, PARTNER, index, partner)

    def to_far(source, index):
        return remote(source, DIRECT, index, far)

    def relay(index):
        return remote(blocks.at[DIRECT], RELAYED, index, partner)

    def to_near(index):
        return remote(blocks.at[PARTNER], SECOND, index, near)

    def each(action, first=0, last=PARTS):
        def run(index, carry):
            action(index)
            return carry
        lax.fori_loop(first, last, run, 0)

    def start_zero(images, texts):
        pl.semaphore_wait(barrier, jnp.where(down_pole, 3 + helpers, 3))
        pl.semaphore_signal(here, inc=1, device_id=(partner,), device_id_type=MESH)
        each(lambda index: to_far(images, index).start())
        each(lambda index: to_partner(texts, index).start())

        @pl.when(down_pole)
        def _():
            for line in range(helpers):
                tell(help_ok, down_helper_at(last_x, line))
            pl.semaphore_wait(helpers_in, helpers)
            tell(help_ok, lax.rem(me - 1 + devices, devices))

    def start_one():
        pl.semaphore_wait(here, 1)
        each(lambda index: to_partner(image_ref, index).start())

    def when(core_is, starts_is, action):
        @pl.when(jnp.logical_and(core == core_is, starts if starts_is else jnp.logical_not(starts)))
        def _():
            action()

    @pl.when(core == 1)
    def _():
        pl.semaphore_wait(barrier, jnp.where(up_helper, 3, 2))
        each(lambda index: to_far(text_ref, index).start())

        @pl.when(up_helper)
        def _():
            tell(helpers_in, down_pole_here)

    for load in loads:
        load.start()

    when(0, False, lambda: start_zero(image_ref, text_ref))
    when(1, False, start_one)
    for load in loads:
        load.wait()
    scale = scale_ref[0]
    bias = bias_ref[0]

    for side in (0, 1):
        losses, coeff = score(own[side], own[1 - side], scale, bias, diagonal=True)
        acc[side] = jnp.dot(coeff, own[1 - side], preferred_element_type=jnp.float32)
        loss[side] = losses

    def follow():
        each(lambda index: to_far(own.at[core], index).wait_send(), 0, PARTS - 1)

        @pl.when(up_pole)
        def _():
            pl.semaphore_wait(help_ok, 1)

        @pl.when(pole)
        def _():
            for line in range(helpers):
                ask(line).start()

        to_near(0).start()
        to_far(own.at[core], PARTS - 1).wait_send()
        each(lambda index: to_near(index).start(), 1, PARTS - 1)

        @pl.when(pole)
        def _():
            short().start()

        @pl.when(jnp.logical_not(jnp.logical_or(pole, up_helper)))
        def _():
            to_near(PARTS - 1).start()

    def carry_over():
        def run(line):
            ask(line).wait_recv()
            lift(line).start()

        on_line(run)

    def pass_on(first=0, last=PARTS):
        def run(index):
            to_far(own.at[core], index).wait_recv()
            relay(index).start()
        each(run, first, last)

    early_images = jnp.logical_and(starts, core == 0)
    late_texts = jnp.logical_and(starts, core == 1)
    late_corner = jnp.logical_and(late_texts, corner)

    when(0, True, lambda: start_zero(own.at[0], own.at[1]))
    when(1, True, start_one)

    def visit(phase, carry):
        @pl.when(jnp.logical_and(up_helper, phase == 1))
        def _():
            carry_over()
            to_near(PARTS - 1).start()

        @pl.when(jnp.logical_and(down_helper, phase == 3))
        def _():
            pl.semaphore_wait(help_ok, 1)
            carry_over()

        slot = jnp.where(late_texts, jnp.where(phase == PARTNER, PARTNER, jnp.where(
            phase == 1, RELAYED, jnp.where((phase == 2) == corner, SECOND, DIRECT))), phase)

        @pl.when(slot == PARTNER)
        def _():
            each(lambda index: to_partner(own.at[1 - core], index).wait_recv())

        @pl.when(jnp.logical_and(slot == DIRECT, jnp.logical_not(early_images)))
        def _():
            pass_on(jnp.where(late_corner, PARTS // 2, 0))

        @pl.when(slot == RELAYED)
        def _():
            each(lambda index: relay(index).wait_recv())

        @pl.when(slot != SECOND)
        def _():
            side = jnp.where(slot == RELAYED, core, 1 - core)
            work(own[side], blocks[slot], acc.at[side], loss.at[side], scale, bias)

        @pl.when(slot == SECOND)
        def _():
            @pl.when(late_corner)
            def _():
                pass_on(0, PARTS // 2)

            half = rows // 2
            each(lambda index: to_near(index).wait_recv(), 0, PARTS // 2)
            work(own[core], second[0:half], acc.at[core], loss.at[core], scale, bias)
            to_near(PARTS // 2).wait_recv()
            work(own[core], second[half:half + part], acc.at[core], loss.at[core], scale, bias)

        @pl.when(phase == 0)
        def _():
            @pl.when(early_images)
            def _():
                pass_on()

            follow()

        return carry

    lax.fori_loop(0, 4, visit, 0)

    def drain(index):
        to_partner(own.at[1 - core], index).wait_send()
        relay(index).wait_send()

    each(drain)
    each(lambda index: to_near(index).wait_send(), 0, PARTS - 1)

    @pl.when(pole)
    def _():
        short().wait_send()
        for line in range(helpers):
            ask(line).wait_send()

    @pl.when(jnp.logical_not(pole))
    def _():
        to_near(PARTS - 1).wait_send()

    @pl.when(helper)
    def _():
        on_line(lambda line: lift(line).wait_send())

    @pl.when(pole)
    def _():
        for line in range(helpers):
            lift(line).wait_recv()
        short().wait_recv()

    @pl.when(jnp.logical_not(pole))
    def _():
        to_near(PARTS - 1).wait_recv()


def finish_kernel(acc, loss, own, second, scale_ref, bias_ref, loss_ref, image_ref, text_ref, row_loss, sems):
    core = lax.rem(lax.axis_index("dp"), 2)
    rows = loss.shape[1]
    tile = rows // TILES
    scale = scale_ref[0]
    bias = bias_ref[0]
    last = second[rows - rows // PARTS:]

    def store(side, target, slot, piece):
        return pltpu.make_async_copy(acc.at[side, piece], target.at[piece], sems.at[slot])

    whole = pl.ds(0, rows)

    def both(action):
        @pl.when(core == 1)
        def _():
            action(image_ref, text_ref)

        @pl.when(core == 0)
        def _():
            action(text_ref, image_ref)

    both(lambda done, open_: store(1 - core, done, TILES, whole).start())
    for index in range(TILES):
        piece = pl.ds(index * tile, tile)
        losses, coeff = score(own[core, piece], last, scale, bias)
        acc[core, piece] += jnp.dot(coeff, last, preferred_element_type=jnp.float32)
        loss[core, piece] += losses
        both(lambda done, open_: store(core, open_, index, piece).start())

    row_loss[...] = jnp.sum(loss[0].T, axis=0, keepdims=True) / (3.0 * rows)
    row_copy = pltpu.make_async_copy(row_loss, loss_ref, sems.at[TILES + 1])
    row_copy.start()
    store(1 - core, image_ref, TILES, whole).wait()
    for index in range(TILES):
        store(core, image_ref, index, pl.ds(index * tile, tile)).wait()
    row_copy.wait()


def body(image_embed, text_embed, logit_scale, logit_bias):
    rows, width = image_embed.shape
    devices = lax.axis_size("dp")
    anywhere = pl.BlockSpec(memory_space=pl.ANY)
    smem = pl.BlockSpec(memory_space=pltpu.SMEM)
    hbm = pl.BlockSpec(memory_space=pltpu.HBM)
    vmem = pl.BlockSpec(memory_space=pltpu.VMEM)
    images, texts = (pltpu.with_memory_space_constraint(a, pltpu.HBM) for a in (image_embed, text_embed))
    state = pl.pallas_call(
        functools.partial(ring_kernel, devices),
        out_shape=(
            pltpu.VMEM((2, rows, width), jnp.float32),
            pltpu.VMEM((2, rows, 128), jnp.float32),
            pltpu.VMEM((2, rows, width), jnp.bfloat16),
            pltpu.VMEM((rows, width), jnp.bfloat16),
        ),
        in_specs=[hbm, hbm, smem, smem],
        out_specs=(vmem, vmem, vmem, vmem),
        scratch_shapes=[
            pltpu.VMEM((3, rows, width), jnp.bfloat16),
            pltpu.VMEM((max(HELP), width), jnp.bfloat16),
            pltpu.SemaphoreType.DMA((2,)),
            pltpu.SemaphoreType.DMA((4, PARTS)),
            pltpu.SemaphoreType.DMA((4, PARTS)),
            pltpu.SemaphoreType.REGULAR,
            pltpu.SemaphoreType.REGULAR,
            pltpu.SemaphoreType.REGULAR,
            pltpu.SemaphoreType.DMA((HEIGHT - 1,)),
            pltpu.SemaphoreType.DMA,
            pltpu.SemaphoreType.DMA,
            pltpu.SemaphoreType.DMA((HEIGHT - 1,)),
        ],
        compiler_params=pltpu.CompilerParams(
            collective_id=0, has_side_effects=True, vmem_limit_bytes=32 << 20),
        name="sigmoid_ring",
    )(images, texts, logit_scale, logit_bias)
    state = [pltpu.with_memory_space_constraint(a, pltpu.VMEM) for a in state]
    row_loss, grad_image, grad_text = pl.pallas_call(
        finish_kernel,
        out_shape=(
            jax.ShapeDtypeStruct((1, rows), jnp.float32),
            jax.ShapeDtypeStruct((rows, width), jnp.float32),
            jax.ShapeDtypeStruct((rows, width), jnp.float32),
        ),
        in_specs=[vmem, vmem, vmem, vmem, smem, smem],
        out_specs=(anywhere, anywhere, anywhere),
        scratch_shapes=[pltpu.VMEM((1, rows), jnp.float32), pltpu.SemaphoreType.DMA((TILES + 2,))],
        compiler_params=pltpu.CompilerParams(vmem_limit_bytes=8 << 20),
        name="finish",
    )(*state, logit_scale, logit_bias)
    return row_loss.reshape(rows), grad_image, grad_text


def solution(mesh):
    in_specs = (P("dp", None), P("dp", None), P(), P())
    out_specs = (P("dp"), P("dp", None), P("dp", None))
    return jax.shard_map(body, mesh=mesh, in_specs=in_specs, out_specs=out_specs, check_vma=False)
```

```python
import functools

import jax
import jax.numpy as jnp
from jax import lax
from jax.experimental import pallas as pl
from jax.experimental.pallas import tpu as pltpu
from jax.sharding import PartitionSpec as P

MESH = pl.DeviceIdType.MESH
PARTS = 4
TILES = 4
WIDTH, HEIGHT, DEPTH = 4, 4, 16
HELP = (64, 16, 16)
NT = (((1,), (1,)), ((), ()))
PARTNER, DIRECT, RELAYED, SECOND = 0, 1, 2, 3


def score(own, other, scale, bias, diagonal=False):
    logits = scale * lax.dot_general(own, other, NT, preferred_element_type=jnp.float32) + bias
    small = jnp.exp(-jnp.abs(logits))
    inverse = 1.0 / (1.0 + small)
    sigmoid = jnp.where(logits >= 0.0, inverse, small * inverse)
    signed = logits
    if diagonal:
        rows = lax.broadcasted_iota(jnp.int32, logits.shape, 0)
        match = lax.broadcasted_iota(jnp.int32, logits.shape, 1) == rows
        sigmoid = sigmoid - jnp.where(match, 1.0, 0.0)
        signed = jnp.where(match, -logits, logits)
    losses = jnp.maximum(signed, 0.0) + jnp.log1p(small)
    total = losses[:, 0:128]
    for first in range(128, losses.shape[1], 128):
        total += losses[:, first:first + 128]
    return total, (scale * sigmoid).astype(jnp.bfloat16)


def work(own, other, acc, loss, scale, bias):
    losses, coeff = score(own, other, scale, bias)
    acc[...] += jnp.dot(coeff, other, preferred_element_type=jnp.float32)
    loss[...] += losses


def ring_kernel(devices, image_ref, text_ref, scale_ref, bias_ref, acc, loss, own, second,
                blocks, extra, load_sem, send, recv, here, helpers_in, help_ok,
                help_send, help_recv, lift_send, lift_recv):
    me = lax.axis_index("dp")
    core = lax.rem(me, 2)
    step = 2 * core - 1
    partner = me - step
    near = lax.rem(me + step + devices, devices)
    far = lax.rem(me + 2 * step + devices, devices)
    rows = own.shape[1]
    part = rows // PARTS

    chip = lax.div(me, 2)
    z = lax.rem(chip, DEPTH)
    y = lax.rem(lax.div(chip, DEPTH), HEIGHT)
    x = lax.div(chip, DEPTH * HEIGHT)
    starts = z == 0
    corner = y == 0

    barrier = pltpu.get_barrier_semaphore()

    def greet(distance):
        pl.semaphore_signal(
            barrier, inc=1, device_id=(lax.rem(me + distance + devices, devices),), device_id_type=MESH)

    greet(2 - core)
    greet(-1 - core)

    @pl.when(core == 1)
    def _():
        greet(-1)

    helpers = HEIGHT - 1
    ends = z == DEPTH - 1
    before = x != WIDTH - 1
    after = x != 0
    up_pole = jnp.logical_and(jnp.logical_and(ends, before), jnp.logical_and(y == helpers, core == 1))
    up_helper = jnp.logical_and(jnp.logical_and(ends, after), jnp.logical_and(y != helpers, core == 1))
    down_pole = jnp.logical_and(jnp.logical_and(starts, after), jnp.logical_and(corner, core == 0))
    down_helper = jnp.logical_and(jnp.logical_and(starts, before), jnp.logical_and(y != 0, core == 0))
    pole = jnp.logical_or(up_pole, down_pole)
    helper = jnp.logical_or(up_helper, down_helper)
    helper_line = jnp.where(core == 1, y, helpers - y)

    def device_at(x, y, z, core):
        return 2 * ((x * HEIGHT + y) * DEPTH + z) + core

    def up_helper_at(x, line):
        return device_at(x, line, DEPTH - 1, 1)

    def down_helper_at(x, line):
        return device_at(x, helpers - line, 0, 0)

    up_pole_here = device_at(x, helpers, DEPTH - 1, 1)
    down_pole_here = device_at(x, 0, 0, 0)
    next_x = lax.rem(x + 1, WIDTH)
    last_x = lax.rem(x + WIDTH - 1, WIDTH)

    def tell(semaphore, device):
        pl.semaphore_signal(semaphore, inc=1, device_id=(device,), device_id_type=MESH)

    @pl.when(down_pole)
    def _():
        for line in range(helpers):
            tell(barrier, up_helper_at(x, line))

    @pl.when(down_helper)
    def _():
        tell(barrier, device_at(next_x, 0, 0, 0))

    def help_rows(line):
        return pl.ds(rows - sum(HELP[line:]), HELP[line])

    def ask(line):
        device = jnp.where(core == 1, up_helper_at(next_x, line), down_helper_at(last_x, line))
        return pltpu.make_async_remote_copy(
            src_ref=blocks.at[PARTNER, help_rows(line)], dst_ref=extra.at[pl.ds(0, HELP[line])],
            send_sem=help_send.at[line], recv_sem=help_recv, device_id=(device,), device_id_type=MESH)

    def lift(line):
        return pltpu.make_async_remote_copy(
            src_ref=extra.at[pl.ds(0, HELP[line])], dst_ref=second.at[help_rows(line)], send_sem=lift_send,
            recv_sem=lift_recv.at[line], device_id=(jnp.where(core == 1, down_pole_here, up_pole_here),),
            device_id_type=MESH)

    def on_line(action):
        for line in range(helpers):
            @pl.when(helper_line == line)
            def _():
                action(line)

    def short():
        piece = pl.ds(rows - part, part - sum(HELP))
        return pltpu.make_async_remote_copy(
            src_ref=blocks.at[PARTNER, piece], dst_ref=second.at[piece], send_sem=send.at[SECOND, PARTS - 1],
            recv_sem=recv.at[SECOND, PARTS - 1], device_id=(near,), device_id_type=MESH)

    loads = [
        pltpu.make_async_copy(source, target, load_sem.at[slot])
        for slot, (source, target) in enumerate(((image_ref, own.at[0]), (text_ref, own.at[1])))
    ]

    def piece_of(index):
        return pl.ds(pl.multiple_of(index * part, part), part)

    def remote(source, way, index, device):
        target = second if way == SECOND else blocks.at[way]
        return pltpu.make_async_remote_copy(
            src_ref=source.at[piece_of(index)], dst_ref=target.at[piece_of(index)],
            send_sem=send.at[way, index], recv_sem=recv.at[way, index],
            device_id=(device,), device_id_type=MESH)

    def to_partner(source, index):
        return remote(source, PARTNER, index, partner)

    def to_far(source, index):
        return remote(source, DIRECT, index, far)

    def relay(index):
        return remote(blocks.at[DIRECT], RELAYED, index, partner)

    def to_near(index):
        return remote(blocks.at[PARTNER], SECOND, index, near)

    def each(action, first=0, last=PARTS):
        def run(index, carry):
            action(index)
            return carry
        lax.fori_loop(first, last, run, 0)

    def start_zero(images, texts):
        pl.semaphore_wait(barrier, jnp.where(down_pole, 3 + helpers, 3))
        pl.semaphore_signal(here, inc=1, device_id=(partner,), device_id_type=MESH)
        each(lambda index: to_far(images, index).start())
        each(lambda index: to_partner(texts, index).start())

        @pl.when(down_pole)
        def _():
            for line in range(helpers):
                tell(help_ok, down_helper_at(last_x, line))
            pl.semaphore_wait(helpers_in, helpers)
            tell(help_ok, lax.rem(me - 1 + devices, devices))

    def start_one():
        pl.semaphore_wait(here, 1)
        each(lambda index: to_partner(image_ref, index).start())

    def when(core_is, starts_is, action):
        @pl.when(jnp.logical_and(core == core_is, starts if starts_is else jnp.logical_not(starts)))
        def _():
            action()

    @pl.when(core == 1)
    def _():
        pl.semaphore_wait(barrier, jnp.where(up_helper, 3, 2))
        each(lambda index: to_far(text_ref, index).start())

        @pl.when(up_helper)
        def _():
            tell(helpers_in, down_pole_here)

    for load in loads:
        load.start()

    when(0, False, lambda: start_zero(image_ref, text_ref))
    when(1, False, start_one)
    for load in loads:
        load.wait()
    scale = scale_ref[0]
    bias = bias_ref[0]

    for side in (0, 1):
        losses, coeff = score(own[side], own[1 - side], scale, bias, diagonal=True)
        acc[side] = jnp.dot(coeff, own[1 - side], preferred_element_type=jnp.float32)
        loss[side] = losses

    def follow():
        each(lambda index: to_far(own.at[core], index).wait_send(), 0, PARTS - 1)

        @pl.when(up_pole)
        def _():
            pl.semaphore_wait(help_ok, 1)

        @pl.when(pole)
        def _():
            for line in range(helpers):
                ask(line).start()

        to_near(0).start()
        to_far(own.at[core], PARTS - 1).wait_send()
        each(lambda index: to_near(index).start(), 1, PARTS - 1)

        @pl.when(pole)
        def _():
            short().start()

        @pl.when(jnp.logical_not(jnp.logical_or(pole, up_helper)))
        def _():
            to_near(PARTS - 1).start()

    def carry_over():
        def run(line):
            ask(line).wait_recv()
            lift(line).start()

        on_line(run)

    def pass_on(first=0, last=PARTS):
        def run(index):
            to_far(own.at[core], index).wait_recv()
            relay(index).start()
        each(run, first, last)

    early_images = jnp.logical_and(starts, core == 0)
    late_texts = jnp.logical_and(starts, core == 1)
    late_corner = jnp.logical_and(late_texts, corner)

    when(0, True, lambda: start_zero(own.at[0], own.at[1]))
    when(1, True, start_one)

    def visit(phase, carry):
        @pl.when(jnp.logical_and(up_helper, phase == 1))
        def _():
            carry_over()
            to_near(PARTS - 1).start()

        @pl.when(jnp.logical_and(down_helper, phase == 3))
        def _():
            pl.semaphore_wait(help_ok, 1)
            carry_over()

        slot = jnp.where(late_texts, jnp.where(phase == PARTNER, PARTNER, jnp.where(
            phase == 1, RELAYED, jnp.where((phase == 2) == corner, SECOND, DIRECT))), phase)

        @pl.when(slot == PARTNER)
        def _():
            each(lambda index: to_partner(own.at[1 - core], index).wait_recv())

        @pl.when(jnp.logical_and(slot == DIRECT, jnp.logical_not(early_images)))
        def _():
            pass_on(jnp.where(late_corner, PARTS // 2, 0))

        @pl.when(slot == RELAYED)
        def _():
            each(lambda index: relay(index).wait_recv())

        @pl.when(slot != SECOND)
        def _():
            side = jnp.where(slot == RELAYED, core, 1 - core)
            work(own[side], blocks[slot], acc.at[side], loss.at[side], scale, bias)

        @pl.when(slot == SECOND)
        def _():
            @pl.when(late_corner)
            def _():
                pass_on(0, PARTS // 2)

            half = rows // 2
            each(lambda index: to_near(index).wait_recv(), 0, PARTS // 2)
            work(own[core], second[0:half], acc.at[core], loss.at[core], scale, bias)
            to_near(PARTS // 2).wait_recv()
            work(own[core], second[half:half + part], acc.at[core], loss.at[core], scale, bias)

        @pl.when(phase == 0)
        def _():
            @pl.when(early_images)
            def _():
                pass_on()

            follow()

        return carry

    lax.fori_loop(0, 4, visit, 0)

    def drain(index):
        to_partner(own.at[1 - core], index).wait_send()
        relay(index).wait_send()

    each(drain)
    each(lambda index: to_near(index).wait_send(), 0, PARTS - 1)

    @pl.when(pole)
    def _():
        short().wait_send()
        for line in range(helpers):
            ask(line).wait_send()

    @pl.when(jnp.logical_not(pole))
    def _():
        to_near(PARTS - 1).wait_send()

    @pl.when(helper)
    def _():
        on_line(lambda line: lift(line).wait_send())

    @pl.when(pole)
    def _():
        for line in range(helpers):
            lift(line).wait_recv()
        short().wait_recv()

    @pl.when(jnp.logical_not(pole))
    def _():
        to_near(PARTS - 1).wait_recv()


def finish_kernel(acc, loss, own, second, scale_ref, bias_ref, loss_ref, image_ref, text_ref, row_loss, sems):
    core = lax.rem(lax.axis_index("dp"), 2)
    rows = loss.shape[1]
    tile = rows // TILES
    scale = scale_ref[0]
    bias = bias_ref[0]
    last = second[rows - rows // PARTS:]

    def store(side, target, slot, piece):
        return pltpu.make_async_copy(acc.at[side, piece], target.at[piece], sems.at[slot])

    whole = pl.ds(0, rows)

    def both(action):
        @pl.when(core == 1)
        def _():
            action(image_ref, text_ref)

        @pl.when(core == 0)
        def _():
            action(text_ref, image_ref)

    both(lambda done, open_: store(1 - core, done, TILES, whole).start())
    for index in range(TILES):
        piece = pl.ds(index * tile, tile)
        losses, coeff = score(own[core, piece], last, scale, bias)
        acc[core, piece] += jnp.dot(coeff, last, preferred_element_type=jnp.float32)
        loss[core, piece] += losses
        both(lambda done, open_: store(core, open_, index, piece).start())

    row_loss[...] = jnp.sum(loss[0].T, axis=0, keepdims=True) / (3.0 * rows)
    row_copy = pltpu.make_async_copy(row_loss, loss_ref, sems.at[TILES + 1])
    row_copy.start()
    store(1 - core, image_ref, TILES, whole).wait()
    for index in range(TILES):
        store(core, image_ref, index, pl.ds(index * tile, tile)).wait()
    row_copy.wait()


def body(image_embed, text_embed, logit_scale, logit_bias):
    rows, width = image_embed.shape
    devices = lax.axis_size("dp")
    anywhere = pl.BlockSpec(memory_space=pl.ANY)
    smem = pl.BlockSpec(memory_space=pltpu.SMEM)
    hbm = pl.BlockSpec(memory_space=pltpu.HBM)
    vmem = pl.BlockSpec(memory_space=pltpu.VMEM)
    images, texts = (pltpu.with_memory_space_constraint(a, pltpu.HBM) for a in (image_embed, text_embed))
    state = pl.pallas_call(
        functools.partial(ring_kernel, devices),
        out_shape=(
            pltpu.VMEM((2, rows, width), jnp.float32),
            pltpu.VMEM((2, rows, 128), jnp.float32),
            pltpu.VMEM((2, rows, width), jnp.bfloat16),
            pltpu.VMEM((rows, width), jnp.bfloat16),
        ),
        in_specs=[hbm, hbm, smem, smem],
        out_specs=(vmem, vmem, vmem, vmem),
        scratch_shapes=[
            pltpu.VMEM((3, rows, width), jnp.bfloat16),
            pltpu.VMEM((max(HELP), width), jnp.bfloat16),
            pltpu.SemaphoreType.DMA((2,)),
            pltpu.SemaphoreType.DMA((4, PARTS)),
            pltpu.SemaphoreType.DMA((4, PARTS)),
            pltpu.SemaphoreType.REGULAR,
            pltpu.SemaphoreType.REGULAR,
            pltpu.SemaphoreType.REGULAR,
            pltpu.SemaphoreType.DMA((HEIGHT - 1,)),
            pltpu.SemaphoreType.DMA,
            pltpu.SemaphoreType.DMA,
            pltpu.SemaphoreType.DMA((HEIGHT - 1,)),
        ],
        compiler_params=pltpu.CompilerParams(
            collective_id=0, has_side_effects=True, vmem_limit_bytes=32 << 20),
        name="sigmoid_ring",
    )(images, texts, logit_scale, logit_bias)
    state = [pltpu.with_memory_space_constraint(a, pltpu.VMEM) for a in state]
    row_loss, grad_image, grad_text = pl.pallas_call(
        finish_kernel,
        out_shape=(
            jax.ShapeDtypeStruct((1, rows), jnp.float32),
            jax.ShapeDtypeStruct((rows, width), jnp.float32),
            jax.ShapeDtypeStruct((rows, width), jnp.float32),
        ),
        in_specs=[vmem, vmem, vmem, vmem, smem, smem],
        out_specs=(anywhere, anywhere, anywhere),
        scratch_shapes=[pltpu.VMEM((1, rows), jnp.float32), pltpu.SemaphoreType.DMA((TILES + 2,))],
        compiler_params=pltpu.CompilerParams(vmem_limit_bytes=8 << 20),
        name="finish",
    )(*state, logit_scale, logit_bias)
    return row_loss.reshape(rows), grad_image, grad_text


def solution(mesh):
    in_specs = (P("dp", None), P("dp", None), P(), P())
    out_specs = (P("dp"), P("dp", None), P("dp", None))
    return jax.shard_map(body, mesh=mesh, in_specs=in_specs, out_specs=out_specs, check_vma=False)
```
